32 devices in a mesh: expert: 4 (over y, x), dp: 8 (over z, core).
Axes of the slice: x: 2, y: 2, z: 4, core: 2. Of those that a mesh axis runs over, the one named last changes fastest.
Arguments:
- tokens: bfloat16 [4096, 1024], P(('expert', 'dp')), may hold values from -6 to 6
- cotangent: bfloat16 [4096, 1024], P(('expert', 'dp')), may hold values from -6 to 6
- route_gates: float32 [4096, 6], P(('expert', 'dp')), may hold values from 0.2 to 1
- expert_ids: int32 [4096, 6], P(('expert', 'dp')), may hold values from 0 to 63, as said below
- replica: int32 [4096, 6], P(('expert', 'dp')), may hold values from 0 to 1
- hot_experts: int32 [4], replicated, may hold values from 0 to 3, as said below
- w_gate: bfloat16 [4, 2, 1024, 768], P('expert'), as said below
- w_up: bfloat16 [4, 2, 1024, 768], P('expert'), as said below
- w_down: bfloat16 [4, 2, 768, 1024], P('expert'), as said below
Outputs:
- layer_out: bfloat16 [4096, 1024], P(('expert', 'dp'))
- grad_tokens: bfloat16 [4096, 1024], P(('expert', 'dp'))
- grad_down: float32 [4, 768, 1024], P('expert', 'dp')
The draws below stay inside these ranges and needn't reach their ends.
Inputs may be any that keep to these rules, and one draw needn't show every extreme that they name: `expert_ids`: each row names 6 different experts. `hot_experts`: names each of the 4 experts once and never its own index. `w_gate`: slot 1 of expert s holds the same matrix as slot 0 of expert hot_experts[s]. `w_up`: slot 1 of expert s holds the same matrix as slot 0 of expert hot_experts[s]. `w_down`: slot 1 of expert s holds the same matrix as slot 0 of expert hot_experts[s].
All inputs are finite; a program needn't handle non-finite values.
Results may differ from the reference program's by a relative error of at most 0.0059.
Values may be sent and summed in bfloat16 or wider, within the bound.
No kernel may reach another device: no remote copies, remote signals or barrier semaphores. Data moves between devices by JAX's collectives and lax.ppermute only.
A program may use at most 64 MiB of HBM per device.

```python
import math
import jax
import jax.numpy as jnp
from jax import lax

D = 1024
FF = 768
ALL_EXPERTS = 64
TOP = 6
TOK_DEV = 128
EXPERTS = 4
CAP = 12
GROUPS = 8
TOKENS = 4096


def hot_table(key):
    order_perm = jax.random.permutation(jax.random.fold_in(key, 11), EXPERTS).astype(jnp.int32)
    following = jnp.roll(order_perm, -1)
    return jnp.zeros((EXPERTS,), jnp.int32).at[order_perm].set(following)


def draw_hot_experts(key, part):
    return hot_table(key)


def draw_expert_ids(key, part):
    key = jax.random.fold_in(key, 5)
    bias_key, noise_key = jax.random.split(key)
    bias_score = jax.random.randint(bias_key, (ALL_EXPERTS,), 0, 1 << 15, dtype=jnp.int32)
    noise_score = jax.random.randint(noise_key, (TOKENS, ALL_EXPERTS), 0, 1 << 16, dtype=jnp.int32)
    full_score = (noise_score + bias_score[None, :]) * ALL_EXPERTS + jnp.arange(ALL_EXPERTS, dtype=jnp.int32)[None, :]
    picked = lax.top_k(full_score, TOP)[1]
    return picked.astype(jnp.int32)


def draw_w_gate(key, part):
    hosted = hot_table(key)
    key = jax.random.fold_in(key, 1)
    base = jax.random.normal(key, (EXPERTS, D, FF), jnp.float32) * D ** (-0.5)
    return jnp.stack([base, base[hosted]], axis=1).astype(jnp.bfloat16)


def draw_w_up(key, part):
    hosted = hot_table(key)
    key = jax.random.fold_in(key, 2)
    base = jax.random.normal(key, (EXPERTS, D, FF), jnp.float32) * D ** (-0.5)
    return jnp.stack([base, base[hosted]], axis=1).astype(jnp.bfloat16)


def draw_w_down(key, part):
    hosted = hot_table(key)
    key = jax.random.fold_in(key, 3)
    base = jax.random.normal(key, (EXPERTS, FF, D), jnp.float32) * FF ** (-0.5)
    return jnp.stack([base, base[hosted]], axis=1).astype(jnp.bfloat16)


def place_ends(array, rng, least, largest):
    longest = array.shape.index(max(array.shape))
    spots = []
    for shift in (0, 1):
        where = [jax.random.randint(jax.random.fold_in(rng, axis), (), 0, length) for axis, length in enumerate(array.shape)]
        where[longest] = (where[longest] + shift) % array.shape[longest]
        spots.append(tuple(where))
    return array.at[spots[0]].set(least).at[spots[1]].set(largest)


def steps_of(key, shape, cuts, low, top_value):
    factor_of = 1.0
    for axis_at, blocks in cuts:
        steps = jax.random.uniform(jax.random.fold_in(jax.random.fold_in(key, 6), axis_at), (blocks,), jnp.float32, low / len(cuts), top_value / len(cuts))
        factor_of = factor_of * jnp.repeat(jnp.exp(steps), shape[axis_at] // blocks).reshape((-1,) + (1,) * (len(shape) - 1 - axis_at))
    return factor_of


def normal_values(stream_key, shape, spread, bound, shards=(), kind=jnp.bfloat16):
    drawn = jax.random.normal(stream_key, shape, jnp.float32) * spread
    if len(shards) > 0:
        drawn = steps_of(stream_key, shape, shards, -0.22, 0.18) * drawn
    return jnp.clip(drawn, min=-bound, max=bound).astype(kind)


def setup_inputs(seed: int = 0) -> dict:
    streams_of = jax.random.split(jax.random.key(seed), 10)
    return {
        "tokens": normal_values(streams_of[0], (TOKENS, D), 1.0, 6.0, ((0, 32),)),
        "cotangent": normal_values(streams_of[1], (TOKENS, D), 1.0, 6.0, ((0, 32),)),
        "route_gates": jnp.clip(jnp.exp(math.log(1.0) - 1.609438 * jax.random.uniform(streams_of[2], (TOKENS, TOP), jnp.float32) ** steps_of(streams_of[2], (TOKENS, TOP), ((0, 32),), -0.2, 0.2)), 0.2, 1.0),
        "expert_ids": draw_expert_ids(jax.random.fold_in(streams_of[9], 71), 0),
        "replica": place_ends(jax.random.randint(streams_of[4], (TOKENS, TOP), 0, 2), jax.random.fold_in(streams_of[4], 1), 0, 1).astype(jnp.int32),
        "hot_experts": draw_hot_experts(jax.random.fold_in(streams_of[9], 71), 0),
        "w_gate": draw_w_gate(jax.random.fold_in(streams_of[9], 71), 0),
        "w_up": draw_w_up(jax.random.fold_in(streams_of[9], 71), 0),
        "w_down": draw_w_down(jax.random.fold_in(streams_of[9], 71), 0),
    }


def copy_ranks(expert_ids, replica, hot_experts, experts, block_rows):
    flat_ids = expert_ids.reshape(-1)
    flat_pick = replica.reshape(-1)
    inside = flat_ids < experts
    matches = (hot_experts[None, :] == flat_ids[:, None]).astype(jnp.int32)
    spare_dev = jnp.sum(matches * jnp.arange(experts, dtype=jnp.int32)[None, :], axis=1)
    target = jnp.where(flat_pick == 1, spare_dev, flat_ids)
    copies = jnp.where(inside, 2 * target + flat_pick, 2 * experts).astype(jnp.int32)
    blocked = copies.reshape(-1, block_rows)
    onehot = (blocked[:, :, None] == jnp.arange(2 * experts + 1, dtype=jnp.int32)[None, None, :]).astype(jnp.int32)
    rank_in = jnp.sum(jnp.cumsum(onehot, axis=1) * onehot, axis=2) - 1
    return copies, inside, rank_in.reshape(-1)


def reference(tokens, cotangent, route_gates, expert_ids, replica, hot_experts, w_gate, w_up, w_down):
    routes_block = TOK_DEV * TOP
    blocks = TOKENS // TOK_DEV
    route_total = TOKENS * TOP
    slot_total = 2 * EXPERTS * CAP
    copies, inside, rank_in = copy_ranks(expert_ids, replica, hot_experts, EXPERTS, routes_block)
    kept_mask = inside & (rank_in < CAP)
    position = jnp.where(kept_mask, copies * CAP + rank_in, slot_total).astype(jnp.int32).reshape(blocks, routes_block)
    local_ids = jnp.arange(routes_block, dtype=jnp.int32)

    def fill_block(where_to):
        return jnp.full((slot_total + 1,), routes_block, jnp.int32).at[where_to].set(local_ids)

    slot_route = jax.vmap(fill_block)(position)[:, :slot_total]
    block_base = (jnp.arange(blocks, dtype=jnp.int32) * routes_block)[:, None]
    global_route = jnp.where(slot_route < routes_block, slot_route + block_base, route_total).astype(jnp.int32)
    padded_x = jnp.concatenate([tokens, jnp.zeros((1, D), tokens.dtype)], axis=0)
    padded_dy = jnp.concatenate([cotangent, jnp.zeros((1, D), cotangent.dtype)], axis=0)
    padded_gates = jnp.concatenate([route_gates.reshape(-1), jnp.zeros((1,), route_gates.dtype)], axis=0)

    def one_copy(carry, copy_index):
        layer_acc, grad_acc, down_acc = carry
        chosen = lax.dynamic_slice_in_dim(global_route, copy_index * CAP, CAP, 1).reshape(-1)
        source = (chosen // TOP).astype(jnp.int32)
        rows_in = padded_x[source]
        gate_row = padded_gates[chosen]
        d_out = (gate_row[:, None] * padded_dy[source].astype(jnp.float32)).astype(jnp.bfloat16)
        target = copy_index // 2
        which_slot = copy_index % 2
        gate_w = w_gate[target, which_slot]
        up_w = w_up[target, which_slot]
        down_w = w_down[target, which_slot]
        gate_pre = jnp.dot(rows_in, gate_w, preferred_element_type=jnp.float32)
        up_pre = jnp.dot(rows_in, up_w, preferred_element_type=jnp.float32)
        sigmoid_g = jax.nn.sigmoid(gate_pre)
        silu_gate = gate_pre * sigmoid_g
        hidden = (silu_gate * up_pre).astype(jnp.bfloat16)
        result = jnp.dot(hidden, down_w, preferred_element_type=jnp.float32).astype(jnp.bfloat16)
        dhidden = jnp.dot(d_out, down_w.T, preferred_element_type=jnp.float32)
        d_gate = (dhidden * up_pre * sigmoid_g * (1.0 + gate_pre * (1.0 - sigmoid_g))).astype(jnp.bfloat16)
        d_up = (dhidden * silu_gate).astype(jnp.bfloat16)
        d_rows = jnp.dot(d_gate, gate_w.T, preferred_element_type=jnp.float32)
        d_rows = (d_rows + jnp.dot(d_up, up_w.T, preferred_element_type=jnp.float32)).astype(jnp.bfloat16)
        owner = jnp.where(which_slot == 0, target, hot_experts[target])
        holder = (jnp.arange(EXPERTS, dtype=jnp.int32) == owner).astype(jnp.float32)
        outer_term = jnp.dot(hidden.T, d_out, preferred_element_type=jnp.float32)
        down_acc = down_acc + holder[:, None, None] * outer_term[None, :, :]
        layer_acc = layer_acc.at[source].add(gate_row[:, None] * result.astype(jnp.float32), mode="drop")
        grad_acc = grad_acc.at[source].add(d_rows.astype(jnp.float32), mode="drop")
        return (layer_acc, grad_acc, down_acc), None

    start_carry = (jnp.zeros((TOKENS, D), jnp.float32), jnp.zeros((TOKENS, D), jnp.float32), jnp.zeros((EXPERTS, FF, D), jnp.float32))
    final_carry, unused = lax.scan(one_copy, start_carry, jnp.arange(2 * EXPERTS, dtype=jnp.int32))
    layer_acc, grad_acc, down_acc = final_carry
    return layer_acc.astype(jnp.bfloat16), grad_acc.astype(jnp.bfloat16), down_acc / GROUPS
```

```python
import functools

import jax
import jax.numpy as jnp
from jax import lax
from jax.experimental import pallas as pl
from jax.experimental.pallas import tpu as pltpu
from jax.sharding import PartitionSpec as P

CAP = 12
PAIR = 2 * CAP
VMEM_LIMIT = 48 * 1024 * 1024
BF16 = jnp.bfloat16
F32 = jnp.float32


def dot(a, b, contract=((1,), (0,))):
    return lax.dot_general(a, b, (contract, ((), ())), preferred_element_type=F32)


def partner(index, step, count):
    if count & (count - 1) == 0:
        return index ^ step
    return (index + step) % count


def source(index, step, count):
    if count & (count - 1) == 0:
        return index ^ step
    return (index - step) % count


def call(kernel, out_shape, flops, moved, **kw):
    return pl.pallas_call(
        kernel,
        out_shape=out_shape,
        compiler_params=pltpu.CompilerParams(vmem_limit_bytes=VMEM_LIMIT),
        cost_estimate=pl.CostEstimate(flops=flops, bytes_accessed=moved, transcendentals=0),
        **kw,
    )


def route_kernel(experts, choices, ids_ref, pick_ref, gates_ref, x_ref, dy_ref, *outs):
    sends, (sel_ref, gsel_ref) = outs[:experts], outs[experts:]
    tok_rows, width = x_ref.shape
    lanes = sel_ref.shape[1]
    me = lax.axis_index("expert")
    lane = lax.broadcasted_iota(jnp.int32, (1, lanes), 1)
    expert_at = jnp.full((1, lanes), -1, jnp.int32)
    slot_at = lane
    for step in range(experts):
        inside = (lane >= step * PAIR) & (lane < (step + 1) * PAIR)
        expert_at = jnp.where(inside, partner(me, step, experts), expert_at)
        slot_at = jnp.where(inside, lane - step * PAIR, slot_at)
    copy_at = jnp.where(slot_at >= CAP, 1, 0)
    rank_at = (slot_at - CAP * copy_at).astype(F32)
    key_at = jnp.where(expert_at < 0, -1, 2 * expert_at + copy_at)
    keys = 2 * ids_ref[...] + pick_ref[...]
    gates = gates_ref[...]
    member = jnp.zeros((tok_rows, lanes), F32)
    weight = jnp.zeros((tok_rows, lanes), F32)
    for k in range(choices):
        hit = keys[:, k : k + 1] == key_at
        member = jnp.where(hit, 1.0, member)
        weight = jnp.where(hit, gates[:, k : k + 1], weight)
    row = lax.broadcasted_iota(jnp.int32, (tok_rows, tok_rows), 0)
    col = lax.broadcasted_iota(jnp.int32, (tok_rows, tok_rows), 1)
    earlier = jnp.where(col < row, 1.0, 0.0).astype(BF16)
    rank = dot(earlier, member.astype(BF16))
    kept = (member > 0.0) & (rank == rank_at)
    select = jnp.where(kept, 1.0, 0.0)
    gated = jnp.where(kept, weight, 0.0)
    sel_ref[...] = select.astype(BF16)
    gsel_ref[...] = gated
    pick = select.T.astype(BF16)
    gate_of = jnp.sum(gated.T, axis=1, keepdims=True)
    rows = dot(pick, x_ref[...]).astype(BF16)
    grads = (gate_of * dot(pick, dy_ref[...])).astype(BF16)
    for step in range(experts):
        at = slice(step * PAIR, (step + 1) * PAIR)
        sends[step][:, :width] = rows[at]
        sends[step][:, width:] = grads[at]


def expert_kernel(experts, *refs):
    blocks, (d_ref, gate_ref, up_ref, down_ref) = refs[:experts], refs[experts : experts + 4]
    outs = refs[experts + 4 : 2 * experts + 4]
    ht_ref, x_s, res_s, grad_s = refs[2 * experts + 4 :]
    at, last = pl.program_id(0), pl.num_programs(0) - 1
    width = x_s.shape[1]

    @pl.when(at == 0)
    def _():
        x_s[...] = jnp.concatenate(
            [b[:, :width].astype(F32) for b in blocks], axis=0
        ).astype(BF16)
        res_s[...] = jnp.zeros_like(res_s)
        grad_s[...] = jnp.zeros_like(grad_s)

    x, d_out = x_s[...], d_ref[...]
    gate_w, up_w, down_w = gate_ref[0, 0], up_ref[0, 0], down_ref[0, 0]
    gate_pre = dot(x, gate_w)
    up_pre = dot(x, up_w)
    sig = jax.nn.sigmoid(gate_pre)
    silu = gate_pre * sig
    hidden = silu * up_pre
    ht_ref[...] = hidden.T.astype(BF16)
    res_s[...] += dot(hidden.astype(BF16), down_w)
    dhidden = dot(d_out, down_w, ((1,), (1,)))
    d_gate = (dhidden * up_pre * sig * (1.0 + gate_pre * (1.0 - sig))).astype(BF16)
    d_up = (dhidden * silu).astype(BF16)
    grad_s[...] += dot(d_gate, gate_w, ((1,), (1,))) + dot(d_up, up_w, ((1,), (1,)))

    @pl.when(at == last)
    def _():
        for step in range(experts):
            rows = pl.ds(step * PAIR, PAIR)
            outs[step][:, :width] = res_s[rows, :].astype(BF16)
            outs[step][:, width:] = grad_s[rows, :].astype(BF16)


def combine_kernel(experts, sel_ref, gsel_ref, *refs):
    blocks, (out_ref, grad_ref) = refs[:experts], refs[experts:]
    width = out_ref.shape[1]
    rows = experts * PAIR
    back = jnp.concatenate([b[...].astype(F32) for b in blocks], axis=0).astype(BF16)
    result, d_rows = back[:, :width], back[:, width:]
    weight = gsel_ref[:, :rows]
    high = weight.astype(BF16)
    rest = weight - high.astype(F32)
    mid = rest.astype(BF16)
    low = (rest - mid.astype(F32)).astype(BF16)
    out_ref[...] = (dot(high, result) + (dot(mid, result) + dot(low, result))).astype(BF16)
    grad_ref[...] = dot(sel_ref[:, :rows], d_rows).astype(BF16)


def outer_kernel(count, scale, *refs):
    hts, ds, (keep_ref, give_ref) = refs[:count], refs[count : 2 * count], refs[2 * count :]
    share = keep_ref.shape[0]
    core = lax.axis_index("dp") % 2
    for out, half in ((keep_ref, core), (give_ref, 1 - core)):
        rows = pl.ds(pl.multiple_of(half * share, 16), share)
        total = dot(hts[0][rows, :], ds[0][...])
        for ht, d in zip(hts[1:], ds[1:]):
            total += dot(ht[rows, :], d[...])
        out[...] = total * scale


def swap(value, axis, count, step):
    return lax.ppermute(value, axis, [(i, partner(i, step, count)) for i in range(count)])


def swap_chip(value, chips, step):
    pairs = [(2 * z + c, 2 * partner(z, step, chips) + c) for z in range(chips) for c in range(2)]
    return lax.ppermute(value, "dp", pairs)


def swap_core(value, groups):
    return lax.ppermute(value, "dp", [(i, i ^ 1) for i in range(groups)])


def slice_kernel(chips, ht_ref, *outs):
    z = lax.axis_index("dp") // 2
    share = outs[0].shape[0]
    for step in range(chips):
        start = pl.multiple_of(partner(z, step, chips) * share, 16)
        outs[step][...] = ht_ref[pl.ds(start, share), :]


def grad_by_rows(ht, d_out, groups):
    chips = groups // 2
    hidden_width, rows = ht.shape
    width = d_out.shape[1]
    share = hidden_width // groups
    ds = [d_out] + [swap_chip(d_out, chips, step) for step in range(1, chips)]
    shape = jax.ShapeDtypeStruct((2 * share, rows), BF16)
    hts = call(
        functools.partial(slice_kernel, chips), [shape] * chips, 0, 4 * hidden_width * rows
    )(ht)
    hts = [hts[0]] + [swap_chip(hts[step], chips, step) for step in range(1, chips)]
    shape = jax.ShapeDtypeStruct((share, width), F32)
    keep, give = call(
        functools.partial(outer_kernel, chips, 1.0 / groups),
        [shape] * 2,
        4 * chips * rows * share * width,
        8 * share * width + 2 * chips * rows * (width + 2 * share),
    )(*hts, *ds)
    return keep + swap_core(give, groups)


def grad_by_sums(ht, d_out, groups):
    total = lax.psum_scatter(dot(ht, d_out), "dp", scatter_dimension=0, tiled=True)
    return total / groups


def on_device(
    tokens, cotangent, route_gates, expert_ids, replica, hot_experts, w_gate, w_up, w_down
):
    del hot_experts
    experts = lax.axis_size("expert")
    groups = lax.axis_size("dp")
    tok_rows, width = tokens.shape
    hidden_width = w_gate.shape[3]
    choices = expert_ids.shape[1]
    rows = experts * PAIR
    lanes = -(-rows // 128) * 128
    block = jax.ShapeDtypeStruct((PAIR, 2 * width), BF16)

    *sends, sel, gsel = call(
        functools.partial(route_kernel, experts, choices),
        [block] * experts
        + [
            jax.ShapeDtypeStruct((tok_rows, lanes), BF16),
            jax.ShapeDtypeStruct((tok_rows, lanes), F32),
        ],
        4 * lanes * tok_rows * width,
        4 * (tok_rows + rows) * width,
    )(expert_ids, replica, route_gates, tokens, cotangent)

    came = [sends[0]] + [swap(sends[s], "expert", experts, s) for s in range(1, experts)]
    d_out = jnp.concatenate([b[:, width:] for b in came], axis=0)

    chunk = 256 if hidden_width % 256 == 0 else hidden_width
    whole = lambda shape: pl.BlockSpec(shape, lambda f: (0,) * len(shape))
    wide = pl.BlockSpec((1, 1, width, chunk), lambda f: (0, 0, 0, f))
    *results, ht = call(
        functools.partial(expert_kernel, experts),
        [block] * experts + [jax.ShapeDtypeStruct((hidden_width, rows), BF16)],
        12 * rows * width * hidden_width,
        6 * width * hidden_width + 12 * rows * width,
        grid=(hidden_width // chunk,),
        in_specs=[whole((PAIR, 2 * width))] * experts
        + [
            whole((rows, width)),
            wide,
            wide,
            pl.BlockSpec((1, 1, chunk, width), lambda f: (0, 0, f, 0)),
        ],
        out_specs=[whole((PAIR, 2 * width))] * experts
        + [pl.BlockSpec((chunk, rows), lambda f: (f, 0))],
        scratch_shapes=[
            pltpu.VMEM((rows, width), BF16),
            pltpu.VMEM((rows, width), F32),
            pltpu.VMEM((rows, width), F32),
        ],
    )(*came, d_out, w_gate, w_up, w_down)

    pairs = experts & (experts - 1) == 0
    home = [results[0]] + [
        swap(results[s], "expert", experts, s if pairs else experts - s) for s in range(1, experts)
    ]
    layer_out, grad_tokens = call(
        functools.partial(combine_kernel, experts),
        [jax.ShapeDtypeStruct((tok_rows, width), BF16)] * 2,
        8 * rows * tok_rows * width,
        4 * (tok_rows + rows) * width,
    )(sel, gsel, *home)

    share = hidden_width // groups
    short = groups in (2, 4, 8, 16) and share % 16 == 0
    grad = (grad_by_rows if short else grad_by_sums)(ht, d_out, groups)
    return layer_out, grad_tokens, grad[None]


def solution(mesh):
    in_specs = (
        P(("expert", "dp"), None),
        P(("expert", "dp"), None),
        P(("expert", "dp"), None),
        P(("expert", "dp"), None),
        P(("expert", "dp"), None),
        P(),
        P("expert", None, None, None),
        P("expert", None, None, None),
        P("expert", None, None, None),
    )
    out_specs = (P(("expert", "dp"), None), P(("expert", "dp"), None), P("expert", "dp", None))
    return jax.shard_map(
        on_device, mesh=mesh, in_specs=in_specs, out_specs=out_specs, check_vma=False
    )
```

```python
import functools

import jax
import jax.numpy as jnp
from jax import lax
from jax.experimental import pallas as pl
from jax.experimental.pallas import tpu as pltpu
from jax.sharding import PartitionSpec as P

CAP = 12
PAIR = 2 * CAP
VMEM_LIMIT = 32 * 1024 * 1024
BF16 = jnp.bfloat16
F32 = jnp.float32
NEAR = pl.BlockSpec(memory_space=pltpu.VMEM)
ANY = pl.BlockSpec(memory_space=pl.ANY)
HBM = pl.BlockSpec(memory_space=pltpu.HBM)


def dot(a, b, contract=((1,), (0,))):
    return lax.dot_general(a, b, (contract, ((), ())), preferred_element_type=F32)


def partner(index, step, count):
    if count & (count - 1) == 0:
        return index ^ step
    return (index + step) % count


def call(kernel, out_shape, flops, moved, **kw):
    return pl.pallas_call(
        kernel,
        out_shape=out_shape,
        compiler_params=pltpu.CompilerParams(vmem_limit_bytes=VMEM_LIMIT),
        cost_estimate=pl.CostEstimate(flops=flops, bytes_accessed=moved, transcendentals=0),
        **kw,
    )


def route_kernel(experts, choices, *refs):
    given, (ids_ref, pick_ref, gates_ref, x_ref, dy_ref, sems) = refs[:5], refs[-6:]
    sends, (sel_ref, gsel_ref) = refs[5 : 5 + experts], refs[5 + experts : -6]
    copies = [
        pltpu.make_async_copy(src, dst, sems.at[i])
        for i, (src, dst) in enumerate(zip(given, (ids_ref, pick_ref, gates_ref, x_ref, dy_ref)))
    ]
    for copy in copies:
        copy.start()
    tok_rows, width = x_ref.shape
    rows = sel_ref.shape[0]
    me = lax.axis_index("expert")
    row = lax.broadcasted_iota(jnp.int32, (rows, tok_rows), 0)
    expert_at = jnp.zeros((rows, tok_rows), jnp.int32)
    slot_at = row
    for step in range(experts):
        inside = (row >= step * PAIR) & (row < (step + 1) * PAIR)
        expert_at = jnp.where(inside, partner(me, step, experts), expert_at)
        slot_at = jnp.where(inside, row - step * PAIR, slot_at)
    copy_at = jnp.where(slot_at >= CAP, 1, 0)
    rank_at = (slot_at - CAP * copy_at).astype(F32)
    key_at = 2 * expert_at + copy_at
    for copy in copies[:3]:
        copy.wait()
    keys = 2 * ids_ref[...] + pick_ref[...]
    gates = gates_ref[...]
    member = jnp.zeros((rows, tok_rows), F32)
    weight = jnp.zeros((rows, tok_rows), F32)
    for k in range(choices):
        hit = keys[k : k + 1, :] == key_at
        member = jnp.where(hit, 1.0, member)
        weight = jnp.where(hit, gates[k : k + 1, :], weight)
    first = lax.broadcasted_iota(jnp.int32, (tok_rows, tok_rows), 0)
    second = lax.broadcasted_iota(jnp.int32, (tok_rows, tok_rows), 1)
    earlier = jnp.where(first < second, 1.0, 0.0).astype(BF16)
    rank = dot(member.astype(BF16), earlier)
    kept = (member > 0.0) & (rank == rank_at)
    select = jnp.where(kept, 1.0, 0.0)
    gated = jnp.where(kept, weight, 0.0)
    sel_ref[...] = select
    gsel_ref[...] = gated
    pick = select.astype(BF16)
    gate_of = jnp.sum(gated, axis=1, keepdims=True)
    copies[3].wait()
    chosen = dot(pick, x_ref[...]).astype(BF16)
    copies[4].wait()
    grads = (gate_of * dot(pick, dy_ref[...])).astype(BF16)
    for step in range(experts):
        at = slice(step * PAIR, (step + 1) * PAIR)
        sends[step][:, :width] = chosen[at]
        sends[step][:, width:] = grads[at]


def weights_kernel(after, gate_hbm, up_hbm, down_hbm, gate_ref, up_ref, down_ref, sems):
    del after
    pairs = ((gate_hbm, gate_ref), (up_hbm, up_ref), (down_hbm, down_ref))
    copies = [
        pltpu.make_async_copy(src.at[0, 0], dst, sems.at[i]) for i, (src, dst) in enumerate(pairs)
    ]
    for copy in copies:
        copy.start()
    for copy in copies:
        copy.wait()


def joined(parts):
    return jnp.concatenate([p.astype(F32) for p in parts], axis=0).astype(BF16)


def join_kernel(experts, after, *refs):
    del after
    blocks, d_ref = refs[:experts], refs[experts]
    d_ref[...] = joined([b[:, d_ref.shape[1] :] for b in blocks])


def expert_kernel(experts, chunk, starts, *refs):
    blocks, (gate_ref, up_ref, down_ref) = refs[:experts], refs[experts : experts + 3]
    outs, hts = refs[experts + 3 : 2 * experts + 3], refs[2 * experts + 3 : -3]
    ht_s, res_s, grad_s = refs[-3:]
    hidden_width, width = down_ref.shape
    x = joined([b[:, :width] for b in blocks])
    d_out = joined([b[:, width:] for b in blocks])
    for start in range(0, hidden_width, chunk):
        at = slice(start, start + chunk)
        gate_w, up_w, down_w = gate_ref[:, at], up_ref[:, at], down_ref[at, :]
        gate_pre = dot(x, gate_w)
        up_pre = dot(x, up_w)
        sig = jax.nn.sigmoid(gate_pre)
        silu = gate_pre * sig
        hidden = silu * up_pre
        ht_s[at, :] = hidden.T.astype(BF16)
        res = dot(hidden.astype(BF16), down_w)
        dhidden = dot(d_out, down_w, ((1,), (1,)))
        d_gate = (dhidden * up_pre * sig * (1.0 + gate_pre * (1.0 - sig))).astype(BF16)
        d_up = (dhidden * silu).astype(BF16)
        grad = dot(d_gate, gate_w, ((1,), (1,))) + dot(d_up, up_w, ((1,), (1,)))
        if start == 0:
            res_s[...] = res
            grad_s[...] = grad
        else:
            res_s[...] += res
            grad_s[...] += grad
    for step in range(experts):
        rows = pl.ds(step * PAIR, PAIR)
        outs[step][:, :width] = res_s[rows, :].astype(BF16)
        outs[step][:, width:] = grad_s[rows, :].astype(BF16)
    for ht, firsts in zip(hts, starts()):
        share = ht.shape[0] // len(firsts)
        for i, first in enumerate(firsts):
            ht[i * share : (i + 1) * share, :] = ht_s[pl.ds(pl.multiple_of(first * share, 16), share), :]


def combine_kernel(experts, after, sel_ref, gsel_ref, *refs):
    del after
    blocks, (out_ref, grad_ref) = refs[:experts], refs[experts:]
    width = out_ref.shape[1]
    back = joined([b[...] for b in blocks])
    result, d_rows = back[:, :width], back[:, width:]
    weight = gsel_ref[...].T
    high = weight.astype(BF16)
    rest = weight - high.astype(F32)
    mid = rest.astype(BF16)
    low = (rest - mid.astype(F32)).astype(BF16)
    out_ref[...] = (dot(high, result) + (dot(mid, result) + dot(low, result))).astype(BF16)
    grad_ref[...] = dot(sel_ref[...].T.astype(BF16), d_rows).astype(BF16)


def pack_kernel(d_ref, far_ref, near_ht, far_ht, *refs):
    pair_ref = refs[-1]
    rows, width = d_ref.shape
    half = near_ht.shape[0] // 2
    pair_ref[:rows] = d_ref[...]
    pair_ref[rows : 2 * rows] = far_ref[...]
    pair_ref[2 * rows :] = jnp.zeros_like(pair_ref[2 * rows :])
    step = pair_ref.shape[0] - 2 * rows
    lanes = width // (2 * half // step)
    for i in range(2 * half // step):
        src, first = (near_ht, i * step) if i * step < half else (far_ht, i * step - half)
        pair_ref[2 * rows :, i * lanes : i * lanes + rows] = src[half + first : half + first + step]


def outer_kernel(scale, d_ref, far_ref, near_ht, far_ht, pair_ref, keep_ref, give_ref):
    rows, width = d_ref.shape
    share = keep_ref.shape[0]
    half = 2 * share
    step = pair_ref.shape[0] - 2 * rows
    count = 2 * half // step
    lanes = width // count
    total = dot(near_ht[:half], d_ref[...]) + dot(far_ht[:half], far_ref[...])
    for i in range(2):
        blocks = range(i * count // 2, (i + 1) * count // 2)
        ht = jnp.concatenate(
            [pair_ref[2 * rows :, k * lanes : k * lanes + rows] for k in blocks], axis=0
        )
        total += dot(ht, pair_ref[i * rows : (i + 1) * rows])
    keep_ref[...] = total[:share] * scale
    give_ref[...] = (total[share:] * scale).astype(BF16)


def swap(value, axis, count, step):
    return lax.ppermute(value, axis, [(i, partner(i, step, count)) for i in range(count)])


CORE, EXCHANGE, FAR = 1, 2, 4
NEAR_UNITS = (0, EXCHANGE, CORE, CORE ^ EXCHANGE)


def gathered_units():
    me = lax.axis_index("dp")
    return [[me ^ unit for unit in NEAR_UNITS], [me ^ FAR ^ unit for unit in NEAR_UNITS]]


def all_units():
    return [[0]]


def grad_by_rows(hts, d_out, home, groups):
    near_ht, far_ht = hts
    rows, width = d_out.shape
    share = near_ht.shape[0] // 4
    far = swap(d_out, "dp", groups, FAR)
    far_ht = swap(far_ht, "dp", groups, FAR)
    extra = near_ht.shape[0] * 128 // width
    pair = call(
        pack_kernel,
        jax.ShapeDtypeStruct((2 * rows + extra, width), BF16),
        0,
        8 * rows * width,
        in_specs=[NEAR] * 4 + [ANY] * len(home),
    )(d_out, far, near_ht, far_ht, *home)
    pair = swap(pair, "dp", groups, CORE)
    keep, give = call(
        functools.partial(outer_kernel, 1.0 / groups),
        [jax.ShapeDtypeStruct((share, width), F32), jax.ShapeDtypeStruct((share, width), BF16)],
        16 * rows * share * width,
        6 * share * width + 8 * rows * (width + 2 * share),
    )(d_out, far, near_ht, far_ht, pair)
    return keep, give


def grad_by_sums(hts, d_out, groups):
    total = lax.psum_scatter(dot(hts[0], d_out), "dp", scatter_dimension=0, tiled=True)
    return total / groups


def on_device(
    tokens, cotangent, route_gates, expert_ids, replica, hot_experts, w_gate, w_up, w_down
):
    del hot_experts
    ids, picks, gates, tokens, cotangent, w_gate, w_up, w_down = (
        pltpu.with_memory_space_constraint(a, pltpu.HBM)
        for a in (
            expert_ids.T, replica.T, route_gates.T, tokens, cotangent, w_gate, w_up, w_down
        )
    )
    experts = lax.axis_size("expert")
    groups = lax.axis_size("dp")
    tok_rows, width = tokens.shape
    hidden_width = w_gate.shape[3]
    choices = expert_ids.shape[1]
    rows = experts * PAIR
    block = jax.ShapeDtypeStruct((PAIR, 2 * width), BF16)

    *sends, sel, gsel = call(
        functools.partial(route_kernel, experts, choices),
        [block] * experts + [jax.ShapeDtypeStruct((rows, tok_rows), F32)] * 2,
        4 * rows * tok_rows * width,
        4 * (tok_rows + rows) * width,
        in_specs=[HBM] * 5,
        scratch_shapes=[
            pltpu.VMEM((choices, tok_rows), jnp.int32),
            pltpu.VMEM((choices, tok_rows), jnp.int32),
            pltpu.VMEM((choices, tok_rows), F32),
            pltpu.VMEM((tok_rows, width), BF16),
            pltpu.VMEM((tok_rows, width), BF16),
            pltpu.SemaphoreType.DMA((5,)),
        ],
    )(ids, picks, gates, tokens, cotangent)

    own_gate, own_up, own_down = call(
        weights_kernel,
        [
            jax.ShapeDtypeStruct((width, hidden_width), BF16),
            jax.ShapeDtypeStruct((width, hidden_width), BF16),
            jax.ShapeDtypeStruct((hidden_width, width), BF16),
        ],
        0,
        12 * width * hidden_width,
        in_specs=[ANY] + [HBM] * 3,
        scratch_shapes=[pltpu.SemaphoreType.DMA((3,))],
    )(gsel, w_gate, w_up, w_down)

    came = [sends[0]] + [swap(sends[s], "expert", experts, s) for s in range(1, experts)]
    d_out = call(
        functools.partial(join_kernel, experts),
        jax.ShapeDtypeStruct((rows, width), BF16),
        0,
        4 * rows * width,
        in_specs=[ANY] + [NEAR] * experts,
    )(own_gate, *came)

    share = hidden_width // groups
    short = groups == 8 and share % 32 == 0 and rows <= 128 and width % 128 == 0
    if short:
        parts = [jax.ShapeDtypeStruct((4 * share, rows), BF16)] * 2
    else:
        parts = [jax.ShapeDtypeStruct((hidden_width, rows), BF16)]
    chunk = 256 if hidden_width % 256 == 0 else hidden_width
    outs = call(
        functools.partial(expert_kernel, experts, chunk, gathered_units if short else all_units),
        [block] * experts + parts,
        12 * rows * width * hidden_width,
        6 * width * hidden_width + 12 * rows * width,
        scratch_shapes=[
            pltpu.VMEM((hidden_width, rows), BF16),
            pltpu.VMEM((rows, width), F32),
            pltpu.VMEM((rows, width), F32),
        ],
    )(*came, own_gate, own_up, own_down)
    results, hts = outs[:experts], outs[experts:]

    pairs = experts & (experts - 1) == 0
    home = [results[0]] + [
        swap(results[s], "expert", experts, s if pairs else experts - s) for s in range(1, experts)
    ]
    if short:
        keep, give = grad_by_rows(hts, d_out, home, groups)
        grad = keep + swap(give, "dp", groups, EXCHANGE).astype(F32)
    else:
        give = sel
        grad = grad_by_sums(hts, d_out, groups)
    layer_out, grad_tokens = call(
        functools.partial(combine_kernel, experts),
        [jax.ShapeDtypeStruct((tok_rows, width), BF16)] * 2,
        8 * rows * tok_rows * width,
        4 * (tok_rows + rows) * width,
        in_specs=[ANY] + [NEAR] * (2 + experts),
    )(give, sel, gsel, *home)
    return layer_out, grad_tokens, grad[None]


def solution(mesh):
    in_specs = (
        P(("expert", "dp"), None),
        P(("expert", "dp"), None),
        P(("expert", "dp"), None),
        P(("expert", "dp"), None),
        P(("expert", "dp"), None),
        P(),
        P("expert", None, None, None),
        P("expert", None, None, None),
        P("expert", None, None, None),
    )
    out_specs = (P(("expert", "dp"), None), P(("expert", "dp"), None), P("expert", "dp", None))
    return jax.shard_map(
        on_device, mesh=mesh, in_specs=in_specs, out_specs=out_specs, check_vma=False
    )
```

```python
import functools

import jax
import jax.numpy as jnp
from jax import lax
from jax.experimental import pallas as pl
from jax.experimental.pallas import tpu as pltpu
from jax.sharding import PartitionSpec as P

CAP = 12
PAIR = 2 * CAP
VMEM_LIMIT = 32 * 1024 * 1024
BF16 = jnp.bfloat16
F32 = jnp.float32
NEAR = pl.BlockSpec(memory_space=pltpu.VMEM)
FLOPS, BYTES = 1.0e9, 3.0e6
ANY = pl.BlockSpec(memory_space=pl.ANY)
HBM = pl.BlockSpec(memory_space=pltpu.HBM)


def dot(a, b, contract=((1,), (0,))):
    return lax.dot_general(a, b, (contract, ((), ())), preferred_element_type=F32)


def partner(index, step, count):
    if count & (count - 1) == 0:
        return index ^ step
    return (index + step) % count


def call(kernel, micros, out_shape, **kw):
    return pl.pallas_call(
        kernel,
        out_shape=out_shape,
        compiler_params=pltpu.CompilerParams(vmem_limit_bytes=VMEM_LIMIT),
        cost_estimate=pl.CostEstimate(
            flops=int(micros * FLOPS), bytes_accessed=int(micros * BYTES), transcendentals=0
        ),
        **kw,
    )


def route_kernel(experts, choices, *refs):
    given, (ids_ref, pick_ref, gates_ref, x_ref, dy_ref, sems) = refs[:5], refs[-6:]
    sends, (sel_ref, gsel_ref) = refs[5 : 5 + experts], refs[5 + experts : -6]
    copies = [
        pltpu.make_async_copy(src, dst, sems.at[i])
        for i, (src, dst) in enumerate(zip(given, (ids_ref, pick_ref, gates_ref, x_ref, dy_ref)))
    ]
    for copy in copies:
        copy.start()
    tok_rows, width = x_ref.shape
    rows = sel_ref.shape[0]
    me = lax.axis_index("expert")
    row = lax.broadcasted_iota(jnp.int32, (rows, tok_rows), 0)
    expert_at = jnp.zeros((rows, tok_rows), jnp.int32)
    slot_at = row
    for step in range(experts):
        inside = (row >= step * PAIR) & (row < (step + 1) * PAIR)
        expert_at = jnp.where(inside, partner(me, step, experts), expert_at)
        slot_at = jnp.where(inside, row - step * PAIR, slot_at)
    copy_at = jnp.where(slot_at >= CAP, 1, 0)
    rank_at = (slot_at - CAP * copy_at).astype(F32)
    key_at = 2 * expert_at + copy_at
    for copy in copies[:3]:
        copy.wait()
    keys = 2 * ids_ref[...] + pick_ref[...]
    gates = gates_ref[...]
    member = jnp.zeros((rows, tok_rows), F32)
    weight = jnp.zeros((rows, tok_rows), F32)
    for k in range(choices):
        hit = keys[k : k + 1, :] == key_at
        member = jnp.where(hit, 1.0, member)
        weight = jnp.where(hit, gates[k : k + 1, :], weight)
    first = lax.broadcasted_iota(jnp.int32, (tok_rows, tok_rows), 0)
    second = lax.broadcasted_iota(jnp.int32, (tok_rows, tok_rows), 1)
    earlier = jnp.where(first < second, 1.0, 0.0).astype(BF16)
    rank = dot(member.astype(BF16), earlier)
    kept = (member > 0.0) & (rank == rank_at)
    select = jnp.where(kept, 1.0, 0.0)
    gated = jnp.where(kept, weight, 0.0)
    sel_ref[...] = select
    gsel_ref[...] = gated
    pick = select.astype(BF16)
    gate_of = jnp.sum(gated, axis=1, keepdims=True)
    copies[3].wait()
    chosen = dot(pick, x_ref[...]).astype(BF16)
    copies[4].wait()
    grads = (gate_of * dot(pick, dy_ref[...])).astype(BF16)
    for step in range(experts):
        at = slice(step * PAIR, (step + 1) * PAIR)
        sends[step][:, :width] = chosen[at]
        sends[step][:, width:] = grads[at]


def weights_kernel(after, gate_hbm, up_hbm, down_hbm, gate_ref, up_ref, down_ref, sems):
    del after
    pairs = ((gate_hbm, gate_ref), (up_hbm, up_ref), (down_hbm, down_ref))
    copies = [
        pltpu.make_async_copy(src.at[0, 0], dst, sems.at[i]) for i, (src, dst) in enumerate(pairs)
    ]
    for copy in copies:
        copy.start()
    for copy in copies:
        copy.wait()


def joined(parts):
    return jnp.concatenate([p.astype(F32) for p in parts], axis=0).astype(BF16)


def join_kernel(experts, after, *refs):
    del after
    blocks, d_ref = refs[:experts], refs[experts]
    d_ref[...] = joined([b[:, d_ref.shape[1] :] for b in blocks])


def forward_kernel(experts, chunk, units_of, after, *refs):
    del after
    blocks, (gate_ref, up_ref), hts = refs[:experts], refs[experts : experts + 2], refs[experts + 2 : -5]
    hidden_ref, dgate_ref, silu_ref, x_s, ht_s = refs[-5:]
    width, hidden_width = gate_ref.shape
    x_s[...] = joined([b[:, :width] for b in blocks])
    for start in range(0, hidden_width, chunk):
        at = slice(start, start + chunk)
        gate_pre = dot(x_s[...], gate_ref[:, at])
        up_pre = dot(x_s[...], up_ref[:, at])
        sig = jax.nn.sigmoid(gate_pre)
        silu = gate_pre * sig
        hidden = silu * up_pre
        ht_s[at, :] = hidden.T.astype(BF16)
        hidden_ref[:, at] = hidden.astype(BF16)
        dgate_ref[:, at] = up_pre * sig * (1.0 + gate_pre * (1.0 - sig))
        silu_ref[:, at] = silu
    for ht, firsts in zip(hts, units_of()):
        share = hidden_width if len(firsts) == 1 else hidden_width // 8
        units = [
            ht_s[pl.ds(pl.multiple_of(first * share, 16), share), :] for first in firsts
        ]
        for i, unit in enumerate(units[: ht.shape[0] // share]):
            if ht.shape[1] > unit.shape[1]:
                more = ht.shape[1] - unit.shape[1]
                unit = beside([unit, units[-1][:, i * more : (i + 1) * more]])
            ht[i * share : (i + 1) * share, :] = unit


def backward_kernel(experts, chunk, *refs):
    blocks, (gate_ref, up_ref, down_ref) = refs[:experts], refs[experts : experts + 3]
    hidden_ref, dgate_ref, silu_ref = refs[experts + 3 : experts + 6]
    outs, (d_s, res_s, grad_s) = refs[experts + 6 : -3], refs[-3:]
    hidden_width, width = down_ref.shape
    d_s[...] = joined([b[:, width:] for b in blocks])
    for start in range(0, hidden_width, chunk):
        at = slice(start, start + chunk)
        gate_w, up_w, down_w = gate_ref[:, at], up_ref[:, at], down_ref[at, :]
        res = dot(hidden_ref[:, at], down_w)
        dhidden = dot(d_s[...], down_w, ((1,), (1,)))
        d_gate = (dhidden * dgate_ref[:, at]).astype(BF16)
        d_up = (dhidden * silu_ref[:, at]).astype(BF16)
        grad = dot(d_gate, gate_w, ((1,), (1,))) + dot(d_up, up_w, ((1,), (1,)))
        if start == 0:
            res_s[...] = res
            grad_s[...] = grad
        else:
            res_s[...] += res
            grad_s[...] += grad
    for step in range(experts):
        rows = pl.ds(step * PAIR, PAIR)
        outs[step][:, :width] = res_s[rows, :].astype(BF16)
        outs[step][:, width:] = grad_s[rows, :].astype(BF16)


def combine_kernel(experts, sel_ref, gsel_ref, *refs):
    blocks, (out_ref, grad_ref) = refs[:experts], refs[experts:]
    width = out_ref.shape[1]
    back = joined([b[...] for b in blocks])
    result, d_rows = back[:, :width], back[:, width:]
    weight = gsel_ref[...].T
    high = weight.astype(BF16)
    rest = weight - high.astype(F32)
    mid = rest.astype(BF16)
    low = (rest - mid.astype(F32)).astype(BF16)
    out_ref[...] = (dot(high, result) + (dot(mid, result) + dot(low, result))).astype(BF16)
    grad_ref[...] = dot(sel_ref[...].T.astype(BF16), d_rows).astype(BF16)


def beside(parts):
    return jnp.concatenate([p.astype(F32) for p in parts], axis=1).astype(BF16)


def pack_kernel(d_ref, far_ref, near_ht, far_ht, after, pair_ref):
    del after
    rows, width = d_ref.shape
    share = near_ht.shape[0] // 4
    pair_ref[:rows] = d_ref[...]
    pair_ref[rows : 2 * rows] = far_ref[...]
    pair_ref[2 * rows :] = jnp.zeros_like(pair_ref[2 * rows :])
    step = pair_ref.shape[0] - 2 * rows
    lanes = width // (4 * share // step)
    last = beside([far_ht[k * share : (k + 1) * share, rows:] for k in range(3)])
    units = [near_ht[2 * share : 3 * share], near_ht[3 * share :], far_ht[2 * share :, :rows], last]
    at = 0
    for unit in units:
        for first in range(0, share, step):
            pair_ref[2 * rows :, at : at + rows] = unit[first : first + step]
            at += lanes


def outer_kernel(scale, near_ht, far_ht, own_ref, pair_ref, *refs):
    keep_ref, give_ref = refs[-2:]
    rows, width = near_ht.shape[1], own_ref.shape[1]
    share = keep_ref.shape[0]
    half = 2 * share
    step = pair_ref.shape[0] - 2 * rows
    count = 2 * half // step
    lanes = width // count
    total = dot(near_ht[:half], own_ref[:rows]) + dot(far_ht[:half, :rows], own_ref[rows : 2 * rows])
    for i in range(2):
        blocks = range(i * count // 2, (i + 1) * count // 2)
        ht = jnp.concatenate(
            [pair_ref[2 * rows :, k * lanes : k * lanes + rows] for k in blocks], axis=0
        )
        total += dot(ht, pair_ref[i * rows : (i + 1) * rows])
    keep_ref[...] = total[:share] * scale
    give_ref[...] = (total[share:] * scale).astype(BF16)


def release_kernel(count, after, *refs):
    del after
    for src, dst in zip(refs[:count], refs[count:]):
        dst[...] = src[...]


def swap(value, axis, count, step):
    return lax.ppermute(value, axis, [(i, partner(i, step, count)) for i in range(count)])


CORE, FAR, EXCHANGE = 1, 2, 4
NEAR_UNITS = (0, EXCHANGE, CORE, CORE ^ EXCHANGE)


def gathered_units():
    me = lax.axis_index("dp")
    return [[me ^ unit for unit in NEAR_UNITS], [me ^ FAR ^ unit for unit in NEAR_UNITS]]


def all_units():
    return [[0]]


def grad_by_rows(hts, d_out, after, groups):
    near_ht, far_ht = hts
    rows, width = d_out.shape
    share = near_ht.shape[0] // 4
    far = swap(d_out, "dp", groups, FAR)
    far_ht = swap(far_ht, "dp", groups, FAR)
    extra = near_ht.shape[0] * 128 // width
    own = call(
        pack_kernel,
        0.2,
        jax.ShapeDtypeStruct((2 * rows + extra, width), BF16),
        in_specs=[NEAR] * 4 + [ANY],
    )(d_out, far, near_ht, far_ht, after)
    pair = swap(own, "dp", groups, CORE)
    return call(
        functools.partial(outer_kernel, 1.0 / groups),
        0.6,
        [jax.ShapeDtypeStruct((share, width), F32), jax.ShapeDtypeStruct((share, width), BF16)],
    )(near_ht, far_ht, own, pair)


def grad_by_sums(hts, d_out, groups):
    total = lax.psum_scatter(dot(hts[0], d_out), "dp", scatter_dimension=0, tiled=True)
    return total / groups


def on_device(
    tokens, cotangent, route_gates, expert_ids, replica, hot_experts, w_gate, w_up, w_down
):
    del hot_experts
    ids, picks, gates, tokens, cotangent, w_gate, w_up, w_down = (
        pltpu.with_memory_space_constraint(a, pltpu.HBM)
        for a in (
            expert_ids.T, replica.T, route_gates.T, tokens, cotangent, w_gate, w_up, w_down
        )
    )
    experts = lax.axis_size("expert")
    groups = lax.axis_size("dp")
    tok_rows, width = tokens.shape
    hidden_width = w_gate.shape[3]
    choices = expert_ids.shape[1]
    rows = experts * PAIR
    block = jax.ShapeDtypeStruct((PAIR, 2 * width), BF16)

    *sends, sel, gsel = call(
        functools.partial(route_kernel, experts, choices),
        1.4,
        [block] * experts + [jax.ShapeDtypeStruct((rows, tok_rows), F32)] * 2,
        in_specs=[HBM] * 5,
        scratch_shapes=[
            pltpu.VMEM((choices, tok_rows), jnp.int32),
            pltpu.VMEM((choices, tok_rows), jnp.int32),
            pltpu.VMEM((choices, tok_rows), F32),
            pltpu.VMEM((tok_rows, width), BF16),
            pltpu.VMEM((tok_rows, width), BF16),
            pltpu.SemaphoreType.DMA((5,)),
        ],
    )(ids, picks, gates, tokens, cotangent)

    own_gate, own_up, own_down = call(
        weights_kernel,
        2.4,
        [
            jax.ShapeDtypeStruct((width, hidden_width), BF16),
            jax.ShapeDtypeStruct((width, hidden_width), BF16),
            jax.ShapeDtypeStruct((hidden_width, width), BF16),
        ],
        in_specs=[ANY] + [HBM] * 3,
        scratch_shapes=[pltpu.SemaphoreType.DMA((3,))],
    )(gsel, w_gate, w_up, w_down)

    came = [sends[0]] + [swap(sends[s], "expert", experts, s) for s in range(1, experts)]
    d_out = call(
        functools.partial(join_kernel, experts),
        0.2,
        jax.ShapeDtypeStruct((rows, width), BF16),
        in_specs=[ANY] + [NEAR] * experts,
    )(own_gate, *came)

    share = hidden_width // groups
    short = groups == 8 and experts == 4 and share % 32 == 0
    if short:
        parts = [
            jax.ShapeDtypeStruct((4 * share, rows), BF16),
            jax.ShapeDtypeStruct((3 * share, rows + rows // 3), BF16),
        ]
    else:
        parts = [jax.ShapeDtypeStruct((hidden_width, rows), BF16)]
    chunk = 256 if hidden_width % 256 == 0 else hidden_width
    factors = [jax.ShapeDtypeStruct((rows, hidden_width), t) for t in (BF16, F32, F32)]
    *hts, hidden, d_gate, silu = call(
        functools.partial(forward_kernel, experts, chunk, gathered_units if short else all_units),
        0.9,
        parts + factors,
        in_specs=[ANY] + [NEAR] * (experts + 2),
        scratch_shapes=[pltpu.VMEM((rows, width), BF16), pltpu.VMEM((hidden_width, rows), BF16)],
    )(d_out, *came, own_gate, own_up)
    own_result, *results = call(
        functools.partial(backward_kernel, experts, chunk),
        2.6,
        [block] * experts,
        scratch_shapes=[
            pltpu.VMEM((rows, width), BF16),
            pltpu.VMEM((rows, width), F32),
            pltpu.VMEM((rows, width), F32),
        ],
    )(*came, own_gate, own_up, own_down, hidden, d_gate, silu)

    if short:
        keep, give = grad_by_rows(hts, d_out, own_result, groups)
        grad = keep + swap(give, "dp", groups, EXCHANGE).astype(F32)
        results = call(
            functools.partial(release_kernel, experts - 1),
            9.0,
            [block] * (experts - 1),
            in_specs=[ANY] + [NEAR] * (experts - 1),
        )(give, *results)
    else:
        grad = grad_by_sums(hts, d_out, groups)

    pairs = experts & (experts - 1) == 0
    home = [own_result] + [
        swap(results[s - 1], "expert", experts, s if pairs else experts - s) for s in range(1, experts)
    ]
    layer_out, grad_tokens = call(
        functools.partial(combine_kernel, experts),
        0.1,
        [jax.ShapeDtypeStruct((tok_rows, width), BF16)] * 2,
    )(sel, gsel, *home)
    return layer_out, grad_tokens, grad[None]


def solution(mesh):
    in_specs = (
        P(("expert", "dp"), None),
        P(("expert", "dp"), None),
        P(("expert", "dp"), None),
        P(("expert", "dp"), None),
        P(("expert", "dp"), None),
        P(),
        P("expert", None, None, None),
        P("expert", None, None, None),
        P("expert", None, None, None),
    )
    out_specs = (P(("expert", "dp"), None), P(("expert", "dp"), None), P("expert", "dp", None))
    return jax.shard_map(
        on_device, mesh=mesh, in_specs=in_specs, out_specs=out_specs, check_vma=False
    )
```

```python
import functools

import jax
import jax.numpy as jnp
from jax import lax
from jax.experimental import pallas as pl
from jax.experimental.pallas import tpu as pltpu
from jax.sharding import PartitionSpec as P

CAP = 12
PAIR = 2 * CAP
VMEM_LIMIT = 32 * 1024 * 1024
BF16 = jnp.bfloat16
F32 = jnp.float32
NEAR = pl.BlockSpec(memory_space=pltpu.VMEM)
FLOPS, BYTES = 1.0e9, 3.0e6
ANY = pl.BlockSpec(memory_space=pl.ANY)
HBM = pl.BlockSpec(memory_space=pltpu.HBM)


def dot(a, b, contract=((1,), (0,))):
    return lax.dot_general(a, b, (contract, ((), ())), preferred_element_type=F32)


def partner(index, step, count):
    if count & (count - 1) == 0:
        return index ^ step
    return (index + step) % count


def call(kernel, micros, out_shape, **kw):
    return pl.pallas_call(
        kernel,
        out_shape=out_shape,
        compiler_params=pltpu.CompilerParams(vmem_limit_bytes=VMEM_LIMIT),
        cost_estimate=pl.CostEstimate(
            flops=int(micros * FLOPS), bytes_accessed=int(micros * BYTES), transcendentals=0
        ),
        **kw,
    )


def route_kernel(experts, choices, *refs):
    given, (ids_ref, pick_ref, gates_ref, x_ref, dy_ref, sems) = refs[:5], refs[-6:]
    sends, (sel_ref, gsel_ref) = refs[5 : 5 + experts], refs[5 + experts : -6]
    copies = [
        pltpu.make_async_copy(src, dst, sems.at[i])
        for i, (src, dst) in enumerate(zip(given, (ids_ref, pick_ref, gates_ref, x_ref, dy_ref)))
    ]
    for copy in copies:
        copy.start()
    tok_rows, width = x_ref.shape
    rows = sel_ref.shape[0]
    me = lax.axis_index("expert")
    row = lax.broadcasted_iota(jnp.int32, (rows, tok_rows), 0)
    expert_at = jnp.zeros((rows, tok_rows), jnp.int32)
    slot_at = row
    for step in range(experts):
        inside = (row >= step * PAIR) & (row < (step + 1) * PAIR)
        expert_at = jnp.where(inside, partner(me, step, experts), expert_at)
        slot_at = jnp.where(inside, row - step * PAIR, slot_at)
    copy_at = jnp.where(slot_at >= CAP, 1, 0)
    rank_at = (slot_at - CAP * copy_at).astype(F32)
    key_at = 2 * expert_at + copy_at
    for copy in copies[:3]:
        copy.wait()
    keys = 2 * ids_ref[...] + pick_ref[...]
    gates = gates_ref[...]
    member = jnp.zeros((rows, tok_rows), F32)
    weight = jnp.zeros((rows, tok_rows), F32)
    for k in range(choices):
        hit = keys[k : k + 1, :] == key_at
        member = jnp.where(hit, 1.0, member)
        weight = jnp.where(hit, gates[k : k + 1, :], weight)
    first = lax.broadcasted_iota(jnp.int32, (tok_rows, tok_rows), 0)
    second = lax.broadcasted_iota(jnp.int32, (tok_rows, tok_rows), 1)
    earlier = jnp.where(first < second, 1.0, 0.0).astype(BF16)
    rank = dot(member.astype(BF16), earlier)
    kept = (member > 0.0) & (rank == rank_at)
    select = jnp.where(kept, 1.0, 0.0)
    gated = jnp.where(kept, weight, 0.0)
    sel_ref[...] = select
    gsel_ref[...] = gated
    pick = select.astype(BF16)
    gate_of = jnp.sum(gated, axis=1, keepdims=True)
    copies[3].wait()
    chosen = dot(pick, x_ref[...]).astype(BF16)
    copies[4].wait()
    grads = (gate_of * dot(pick, dy_ref[...])).astype(BF16)
    for step in range(experts):
        at = slice(step * PAIR, (step + 1) * PAIR)
        sends[step][:, :width] = chosen[at]
        sends[step][:, width:] = grads[at]


def weights_kernel(sel_ref, gsel_ref, gate_hbm, up_hbm, down_hbm, *refs):
    gate_ref, up_ref, down_ref, pick_ref, high_ref, mid_ref, low_ref, sems = refs
    pairs = ((gate_hbm, gate_ref), (up_hbm, up_ref), (down_hbm, down_ref))
    copies = [
        pltpu.make_async_copy(src.at[0, 0], dst, sems.at[i]) for i, (src, dst) in enumerate(pairs)
    ]
    for copy in copies:
        copy.start()
    pick_ref[...] = sel_ref[...].T.astype(BF16)
    weight = gsel_ref[...].T
    high = weight.astype(BF16)
    rest = weight - high.astype(F32)
    mid = rest.astype(BF16)
    high_ref[...] = high
    mid_ref[...] = mid
    low_ref[...] = (rest - mid.astype(F32)).astype(BF16)
    for copy in copies:
        copy.wait()


def joined(parts):
    return jnp.concatenate([p.astype(F32) for p in parts], axis=0).astype(BF16)


def join_kernel(experts, after, *refs):
    del after
    blocks, d_ref = refs[:experts], refs[experts]
    d_ref[...] = joined([b[:, d_ref.shape[1] :] for b in blocks])


def forward_kernel(experts, chunk, units_of, after, *refs):
    del after
    blocks, (gate_ref, up_ref), hts = refs[:experts], refs[experts : experts + 2], refs[experts + 2 : -5]
    hidden_ref, dgate_ref, silu_ref, x_s, ht_s = refs[-5:]
    width, hidden_width = gate_ref.shape
    x_s[...] = joined([b[:, :width] for b in blocks])
    for start in range(0, hidden_width, chunk):
        at = slice(start, start + chunk)
        gate_pre = dot(x_s[...], gate_ref[:, at])
        up_pre = dot(x_s[...], up_ref[:, at])
        sig = jax.nn.sigmoid(gate_pre)
        silu = gate_pre * sig
        hidden = silu * up_pre
        ht_s[at, :] = hidden.T.astype(BF16)
        hidden_ref[:, at] = hidden.astype(BF16)
        dgate_ref[:, at] = up_pre * sig * (1.0 + gate_pre * (1.0 - sig))
        silu_ref[:, at] = silu
    for ht, firsts in zip(hts, units_of()):
        share = hidden_width if len(firsts) == 1 else hidden_width // 8
        units = [
            ht_s[pl.ds(pl.multiple_of(first * share, 16), share), :] for first in firsts
        ]
        for i, unit in enumerate(units[: ht.shape[0] // share]):
            if ht.shape[1] > unit.shape[1]:
                more = ht.shape[1] - unit.shape[1]
                unit = beside([unit, units[-1][:, i * more : (i + 1) * more]])
            ht[i * share : (i + 1) * share, :] = unit


def backward_kernel(experts, chunk, *refs):
    blocks, (gate_ref, up_ref, down_ref) = refs[:experts], refs[experts : experts + 3]
    hidden_ref, dgate_ref, silu_ref = refs[experts + 3 : experts + 6]
    outs, (d_s, res_s, grad_s) = refs[experts + 6 : -3], refs[-3:]
    hidden_width, width = down_ref.shape
    d_s[...] = joined([b[:, width:] for b in blocks])
    for start in range(0, hidden_width, chunk):
        at = slice(start, start + chunk)
        gate_w, up_w, down_w = gate_ref[:, at], up_ref[:, at], down_ref[at, :]
        res = dot(hidden_ref[:, at], down_w)
        dhidden = dot(d_s[...], down_w, ((1,), (1,)))
        d_gate = (dhidden * dgate_ref[:, at]).astype(BF16)
        d_up = (dhidden * silu_ref[:, at]).astype(BF16)
        grad = dot(d_gate, gate_w, ((1,), (1,))) + dot(d_up, up_w, ((1,), (1,)))
        if start == 0:
            res_s[...] = res
            grad_s[...] = grad
        else:
            res_s[...] += res
            grad_s[...] += grad
    for step in range(experts):
        rows = pl.ds(step * PAIR, PAIR)
        outs[step][:, :width] = res_s[rows, :].astype(BF16)
        outs[step][:, width:] = grad_s[rows, :].astype(BF16)


def combine_kernel(experts, pick_ref, high_ref, mid_ref, low_ref, *refs):
    blocks, (out_ref, grad_ref) = refs[:experts], refs[experts:]
    width = out_ref.shape[1]
    back = joined([b[...] for b in blocks])
    result, d_rows = back[:, :width], back[:, width:]
    total = dot(mid_ref[...], result) + dot(low_ref[...], result)
    out_ref[...] = (dot(high_ref[...], result) + total).astype(BF16)
    grad_ref[...] = dot(pick_ref[...], d_rows).astype(BF16)


def beside(parts):
    return jnp.concatenate([p.astype(F32) for p in parts], axis=1).astype(BF16)


def pack_kernel(d_ref, far_ref, near_ht, far_ht, after, pair_ref):
    del after
    rows, width = d_ref.shape
    share = near_ht.shape[0] // 4
    pair_ref[:rows] = d_ref[...]
    pair_ref[rows : 2 * rows] = far_ref[...]
    pair_ref[2 * rows :] = jnp.zeros_like(pair_ref[2 * rows :])
    step = pair_ref.shape[0] - 2 * rows
    lanes = width // (4 * share // step)
    last = beside([far_ht[k * share : (k + 1) * share, rows:] for k in range(3)])
    units = [near_ht[2 * share : 3 * share], near_ht[3 * share :], far_ht[2 * share :, :rows], last]
    at = 0
    for unit in units:
        for first in range(0, share, step):
            pair_ref[2 * rows :, at : at + rows] = unit[first : first + step]
            at += lanes


def outer_kernel(scale, near_ht, far_ht, own_ref, pair_ref, *refs):
    keep_ref, give_ref = refs[-2:]
    rows, width = near_ht.shape[1], own_ref.shape[1]
    share = keep_ref.shape[0]
    half = 2 * share
    step = pair_ref.shape[0] - 2 * rows
    count = 2 * half // step
    lanes = width // count
    total = dot(near_ht[:half], own_ref[:rows]) + dot(far_ht[:half, :rows], own_ref[rows : 2 * rows])
    for i in range(2):
        blocks = range(i * count // 2, (i + 1) * count // 2)
        ht = jnp.concatenate(
            [pair_ref[2 * rows :, k * lanes : k * lanes + rows] for k in blocks], axis=0
        )
        total += dot(ht, pair_ref[i * rows : (i + 1) * rows])
    keep_ref[...] = total[:share] * scale
    give_ref[...] = (total[share:] * scale).astype(BF16)


def release_kernel(count, after, *refs):
    del after
    for src, dst in zip(refs[:count], refs[count:]):
        dst[...] = src[...]


def swap(value, axis, count, step):
    return lax.ppermute(value, axis, [(i, partner(i, step, count)) for i in range(count)])


CORE, FAR, EXCHANGE = 1, 2, 6
NEAR_UNITS = (0, EXCHANGE, CORE, CORE ^ EXCHANGE)


def gathered_units():
    me = lax.axis_index("dp")
    return [[me ^ unit for unit in NEAR_UNITS], [me ^ FAR ^ unit for unit in NEAR_UNITS]]


def all_units():
    return [[0]]


def grad_by_rows(hts, d_out, after, groups):
    near_ht, far_ht = hts
    rows, width = d_out.shape
    share = near_ht.shape[0] // 4
    far = swap(d_out, "dp", groups, FAR)
    far_ht = swap(far_ht, "dp", groups, FAR)
    extra = near_ht.shape[0] * 128 // width
    own = call(
        pack_kernel,
        0.2,
        jax.ShapeDtypeStruct((2 * rows + extra, width), BF16),
        in_specs=[NEAR] * 4 + [ANY],
    )(d_out, far, near_ht, far_ht, after)
    pair = swap(own, "dp", groups, CORE)
    return call(
        functools.partial(outer_kernel, 1.0 / groups),
        0.6,
        [jax.ShapeDtypeStruct((share, width), F32), jax.ShapeDtypeStruct((share, width), BF16)],
    )(near_ht, far_ht, own, pair)


def grad_by_sums(hts, d_out, groups):
    total = lax.psum_scatter(dot(hts[0], d_out), "dp", scatter_dimension=0, tiled=True)
    return total / groups


def on_device(
    tokens, cotangent, route_gates, expert_ids, replica, hot_experts, w_gate, w_up, w_down
):
    del hot_experts
    ids, picks, gates, tokens, cotangent, w_gate, w_up, w_down = (
        pltpu.with_memory_space_constraint(a, pltpu.HBM)
        for a in (
            expert_ids.T, replica.T, route_gates.T, tokens, cotangent, w_gate, w_up, w_down
        )
    )
    experts = lax.axis_size("expert")
    groups = lax.axis_size("dp")
    tok_rows, width = tokens.shape
    hidden_width = w_gate.shape[3]
    choices = expert_ids.shape[1]
    rows = experts * PAIR
    block = jax.ShapeDtypeStruct((PAIR, 2 * width), BF16)

    *sends, sel, gsel = call(
        functools.partial(route_kernel, experts, choices),
        1.4,
        [block] * experts + [jax.ShapeDtypeStruct((rows, tok_rows), F32)] * 2,
        in_specs=[HBM] * 5,
        scratch_shapes=[
            pltpu.VMEM((choices, tok_rows), jnp.int32),
            pltpu.VMEM((choices, tok_rows), jnp.int32),
            pltpu.VMEM((choices, tok_rows), F32),
            pltpu.VMEM((tok_rows, width), BF16),
            pltpu.VMEM((tok_rows, width), BF16),
            pltpu.SemaphoreType.DMA((5,)),
        ],
    )(ids, picks, gates, tokens, cotangent)

    own_gate, own_up, own_down, *factors = call(
        weights_kernel,
        2.4,
        [
            jax.ShapeDtypeStruct((width, hidden_width), BF16),
            jax.ShapeDtypeStruct((width, hidden_width), BF16),
            jax.ShapeDtypeStruct((hidden_width, width), BF16),
        ]
        + [jax.ShapeDtypeStruct((tok_rows, rows), BF16)] * 4,
        in_specs=[NEAR] * 2 + [HBM] * 3,
        scratch_shapes=[pltpu.SemaphoreType.DMA((3,))],
    )(sel, gsel, w_gate, w_up, w_down)

    came = [sends[0]] + [swap(sends[s], "expert", experts, s) for s in range(1, experts)]
    d_out = call(
        functools.partial(join_kernel, experts),
        0.2,
        jax.ShapeDtypeStruct((rows, width), BF16),
        in_specs=[ANY] + [NEAR] * experts,
    )(own_gate, *came)

    share = hidden_width // groups
    short = groups == 8 and experts == 4 and share % 32 == 0
    if short:
        parts = [
            jax.ShapeDtypeStruct((4 * share, rows), BF16),
            jax.ShapeDtypeStruct((3 * share, rows + rows // 3), BF16),
        ]
    else:
        parts = [jax.ShapeDtypeStruct((hidden_width, rows), BF16)]
    chunk = 256 if hidden_width % 256 == 0 else hidden_width
    kept = [jax.ShapeDtypeStruct((rows, hidden_width), t) for t in (BF16, F32, F32)]
    *hts, hidden, d_gate, silu = call(
        functools.partial(forward_kernel, experts, chunk, gathered_units if short else all_units),
        0.9,
        parts + kept,
        in_specs=[ANY] + [NEAR] * (experts + 2),
        scratch_shapes=[pltpu.VMEM((rows, width), BF16), pltpu.VMEM((hidden_width, rows), BF16)],
    )(d_out, *came, own_gate, own_up)
    own_result, near_result, *results = call(
        functools.partial(backward_kernel, experts, chunk),
        2.6,
        [block] * experts,
        scratch_shapes=[
            pltpu.VMEM((rows, width), BF16),
            pltpu.VMEM((rows, width), F32),
            pltpu.VMEM((rows, width), F32),
        ],
    )(*came, own_gate, own_up, own_down, hidden, d_gate, silu)

    if short:
        keep, give = grad_by_rows(hts, d_out, own_result, groups)
        grad = keep + swap(give, "dp", groups, EXCHANGE).astype(F32)
        results = call(
            functools.partial(release_kernel, experts - 2),
            9.0,
            [block] * (experts - 2),
            in_specs=[ANY] + [NEAR] * (experts - 2),
        )(give, *results)
    else:
        grad = grad_by_sums(hts, d_out, groups)

    pairs = experts & (experts - 1) == 0
    results = [near_result, *results]
    home = [own_result] + [
        swap(results[s - 1], "expert", experts, s if pairs else experts - s) for s in range(1, experts)
    ]
    layer_out, grad_tokens = call(
        functools.partial(combine_kernel, experts),
        0.1,
        [jax.ShapeDtypeStruct((tok_rows, width), BF16)] * 2,
    )(*factors, *home)
    return layer_out, grad_tokens, grad[None]


def solution(mesh):
    in_specs = (
        P(("expert", "dp"), None),
        P(("expert", "dp"), None),
        P(("expert", "dp"), None),
        P(("expert", "dp"), None),
        P(("expert", "dp"), None),
        P(),
        P("expert", None, None, None),
        P("expert", None, None, None),
        P("expert", None, None, None),
    )
    out_specs = (P(("expert", "dp"), None), P(("expert", "dp"), None), P("expert", "dp", None))
    return jax.shard_map(
        on_device, mesh=mesh, in_specs=in_specs, out_specs=out_specs, check_vma=False
    )
```

```python
import functools

import jax
import jax.numpy as jnp
from jax import lax
from jax.experimental import pallas as pl
from jax.experimental.pallas import tpu as pltpu
from jax.sharding import PartitionSpec as P

CAP = 12
PAIR = 2 * CAP
VMEM_LIMIT = 32 * 1024 * 1024
BF16 = jnp.bfloat16
F32 = jnp.float32
NEAR = pl.BlockSpec(memory_space=pltpu.VMEM)
FLOPS, BYTES = 1.0e9, 3.0e6
ANY = pl.BlockSpec(memory_space=pl.ANY)
HBM = pl.BlockSpec(memory_space=pltpu.HBM)


def dot(a, b, contract=((1,), (0,))):
    return lax.dot_general(a, b, (contract, ((), ())), preferred_element_type=F32)


def partner(index, step, count):
    if count & (count - 1) == 0:
        return index ^ step
    return (index + step) % count


def call(kernel, micros, out_shape, **kw):
    return pl.pallas_call(
        kernel,
        out_shape=out_shape,
        compiler_params=pltpu.CompilerParams(vmem_limit_bytes=VMEM_LIMIT),
        cost_estimate=pl.CostEstimate(
            flops=int(micros * FLOPS), bytes_accessed=int(micros * BYTES), transcendentals=0
        ),
        **kw,
    )


def route_kernel(experts, choices, *refs):
    given, (ids_ref, pick_ref, gates_ref, x_ref, dy_ref, sems) = refs[:5], refs[-6:]
    sends, (sel_ref, gsel_ref) = refs[5 : 5 + experts], refs[5 + experts : -6]
    copies = [
        pltpu.make_async_copy(src, dst, sems.at[i])
        for i, (src, dst) in enumerate(zip(given, (ids_ref, pick_ref, gates_ref, x_ref, dy_ref)))
    ]
    for copy in copies:
        copy.start()
    tok_rows, width = x_ref.shape
    rows = sel_ref.shape[0]
    me = lax.axis_index("expert")
    row = lax.broadcasted_iota(jnp.int32, (rows, tok_rows), 0)
    expert_at = jnp.zeros((rows, tok_rows), jnp.int32)
    slot_at = row
    for step in range(experts):
        inside = (row >= step * PAIR) & (row < (step + 1) * PAIR)
        expert_at = jnp.where(inside, partner(me, step, experts), expert_at)
        slot_at = jnp.where(inside, row - step * PAIR, slot_at)
    copy_at = jnp.where(slot_at >= CAP, 1, 0)
    rank_at = (slot_at - CAP * copy_at).astype(F32)
    key_at = 2 * expert_at + copy_at
    for copy in copies[:3]:
        copy.wait()
    keys = 2 * ids_ref[...] + pick_ref[...]
    gates = gates_ref[...]
    member = jnp.zeros((rows, tok_rows), F32)
    weight = jnp.zeros((rows, tok_rows), F32)
    for k in range(choices):
        hit = keys[k : k + 1, :] == key_at
        member = jnp.where(hit, 1.0, member)
        weight = jnp.where(hit, gates[k : k + 1, :], weight)
    first = lax.broadcasted_iota(jnp.int32, (tok_rows, tok_rows), 0)
    second = lax.broadcasted_iota(jnp.int32, (tok_rows, tok_rows), 1)
    earlier = jnp.where(first < second, 1.0, 0.0).astype(BF16)
    rank = dot(member.astype(BF16), earlier)
    kept = (member > 0.0) & (rank == rank_at)
    select = jnp.where(kept, 1.0, 0.0)
    gated = jnp.where(kept, weight, 0.0)
    sel_ref[...] = select
    gsel_ref[...] = gated
    pick = select.astype(BF16)
    gate_of = jnp.sum(gated, axis=1, keepdims=True)
    copies[3].wait()
    chosen = dot(pick, x_ref[...]).astype(BF16)
    copies[4].wait()
    grads = (gate_of * dot(pick, dy_ref[...])).astype(BF16)
    for step in range(experts):
        at = slice(step * PAIR, (step + 1) * PAIR)
        sends[step][:, :width] = chosen[at]
        sends[step][:, width:] = grads[at]


def weights_kernel(sel_ref, gsel_ref, gate_hbm, up_hbm, down_hbm, *refs):
    gate_ref, up_ref, down_ref, pick_ref, high_ref, mid_ref, low_ref, sems = refs
    pairs = ((gate_hbm, gate_ref), (up_hbm, up_ref), (down_hbm, down_ref))
    copies = [
        pltpu.make_async_copy(src.at[0, 0], dst, sems.at[i]) for i, (src, dst) in enumerate(pairs)
    ]
    for copy in copies:
        copy.start()
    pick_ref[...] = sel_ref[...].T.astype(BF16)
    weight = gsel_ref[...].T
    high = weight.astype(BF16)
    rest = weight - high.astype(F32)
    mid = rest.astype(BF16)
    high_ref[...] = high
    mid_ref[...] = mid
    low_ref[...] = (rest - mid.astype(F32)).astype(BF16)
    for copy in copies:
        copy.wait()


def joined(parts):
    return jnp.concatenate([p.astype(F32) for p in parts], axis=0).astype(BF16)


def join_kernel(experts, after, *refs):
    del after
    blocks, d_ref = refs[:experts], refs[experts]
    d_ref[...] = joined([b[:, d_ref.shape[1] :] for b in blocks])


def forward_kernel(experts, chunk, units_of, after, *refs):
    del after
    blocks, (gate_ref, up_ref), hts = refs[:experts], refs[experts : experts + 2], refs[experts + 2 : -5]
    hidden_ref, dgate_ref, silu_ref, x_s, ht_s = refs[-5:]
    width, hidden_width = gate_ref.shape
    x_s[...] = joined([b[:, :width] for b in blocks])
    for start in range(0, hidden_width, chunk):
        at = slice(start, start + chunk)
        gate_pre = dot(x_s[...], gate_ref[:, at])
        up_pre = dot(x_s[...], up_ref[:, at])
        sig = jax.nn.sigmoid(gate_pre)
        silu = gate_pre * sig
        hidden = silu * up_pre
        ht_s[at, :] = hidden.T.astype(BF16)
        hidden_ref[:, at] = hidden.astype(BF16)
        dgate_ref[:, at] = up_pre * sig * (1.0 + gate_pre * (1.0 - sig))
        silu_ref[:, at] = silu
    for ht, firsts in zip(hts, units_of()):
        share = hidden_width if len(firsts) == 1 else hidden_width // 8
        units = [
            ht_s[pl.ds(pl.multiple_of(first * share, 16), share), :] for first in firsts
        ]
        for i, unit in enumerate(units[: ht.shape[0] // share]):
            if ht.shape[1] > unit.shape[1]:
                more = ht.shape[1] - unit.shape[1]
                unit = beside([unit, units[-1][:, i * more : (i + 1) * more]])
            ht[i * share : (i + 1) * share, :] = unit


def backward_kernel(experts, chunk, *refs):
    blocks, (gate_ref, up_ref, down_ref) = refs[:experts], refs[experts : experts + 3]
    hidden_ref, dgate_ref, silu_ref = refs[experts + 3 : experts + 6]
    outs, (d_s, res_s, grad_s) = refs[experts + 6 : -3], refs[-3:]
    hidden_width, width = down_ref.shape
    d_s[...] = joined([b[:, width:] for b in blocks])
    for start in range(0, hidden_width, chunk):
        at = slice(start, start + chunk)
        gate_w, up_w, down_w = gate_ref[:, at], up_ref[:, at], down_ref[at, :]
        res = dot(hidden_ref[:, at], down_w)
        dhidden = dot(d_s[...], down_w, ((1,), (1,)))
        d_gate = (dhidden * dgate_ref[:, at]).astype(BF16)
        d_up = (dhidden * silu_ref[:, at]).astype(BF16)
        grad = dot(d_gate, gate_w, ((1,), (1,))) + dot(d_up, up_w, ((1,), (1,)))
        if start == 0:
            res_s[...] = res
            grad_s[...] = grad
        else:
            res_s[...] += res
            grad_s[...] += grad
    for step in range(experts):
        rows = pl.ds(step * PAIR, PAIR)
        outs[step][:, :width] = res_s[rows, :].astype(BF16)
        outs[step][:, width:] = grad_s[rows, :].astype(BF16)


def combine_kernel(experts, pick_ref, high_ref, mid_ref, low_ref, *refs):
    blocks, (out_ref, grad_ref) = refs[:experts], refs[experts:]
    width = out_ref.shape[1]
    back = joined([b[...] for b in blocks])
    result, d_rows = back[:, :width], back[:, width:]
    total = dot(mid_ref[...], result) + dot(low_ref[...], result)
    out_ref[...] = (dot(high_ref[...], result) + total).astype(BF16)
    grad_ref[...] = dot(pick_ref[...], d_rows).astype(BF16)


def beside(parts):
    return jnp.concatenate([p.astype(F32) for p in parts], axis=1).astype(BF16)


def pack_kernel(d_ref, far_ref, near_ht, far_ht, after, pair_ref):
    del after
    rows, width = d_ref.shape
    share = near_ht.shape[0] // 4
    pair_ref[:rows] = d_ref[...]
    pair_ref[rows : 2 * rows] = far_ref[...]
    pair_ref[2 * rows :] = jnp.zeros_like(pair_ref[2 * rows :])
    step = pair_ref.shape[0] - 2 * rows
    lanes = width // (4 * share // step)
    last = beside([far_ht[k * share : (k + 1) * share, rows:] for k in range(3)])
    units = [near_ht[2 * share : 3 * share], near_ht[3 * share :], far_ht[2 * share :, :rows], last]
    at = 0
    for unit in units:
        for first in range(0, share, step):
            pair_ref[2 * rows :, at : at + rows] = unit[first : first + step]
            at += lanes


def outer_kernel(scale, near_ht, far_ht, own_ref, pair_ref, *refs):
    keep_ref, give_ref = refs[-2:]
    rows, width = near_ht.shape[1], own_ref.shape[1]
    share = keep_ref.shape[0]
    half = 2 * share
    step = pair_ref.shape[0] - 2 * rows
    count = 2 * half // step
    lanes = width // count
    total = dot(near_ht[:half], own_ref[:rows]) + dot(far_ht[:half, :rows], own_ref[rows : 2 * rows])
    for i in range(2):
        blocks = range(i * count // 2, (i + 1) * count // 2)
        ht = jnp.concatenate(
            [pair_ref[2 * rows :, k * lanes : k * lanes + rows] for k in blocks], axis=0
        )
        total += dot(ht, pair_ref[i * rows : (i + 1) * rows])
    keep_ref[...] = total[:share] * scale
    give_ref[...] = (total[share:] * scale).astype(BF16)


def release_kernel(count, after, *refs):
    del after
    for src, dst in zip(refs[:count], refs[count:]):
        dst[...] = src[...]


def swap(value, axis, count, step):
    return lax.ppermute(value, axis, [(i, partner(i, step, count)) for i in range(count)])


HELD = (2,)

CORE, FAR, EXCHANGE = 1, 2, 6
NEAR_UNITS = (0, EXCHANGE, CORE, CORE ^ EXCHANGE)


def gathered_units():
    me = lax.axis_index("dp")
    return [[me ^ unit for unit in NEAR_UNITS], [me ^ FAR ^ unit for unit in NEAR_UNITS]]


def all_units():
    return [[0]]


def grad_by_rows(hts, d_out, after, groups):
    near_ht, far_ht = hts
    rows, width = d_out.shape
    share = near_ht.shape[0] // 4
    far = swap(d_out, "dp", groups, FAR)
    far_ht = swap(far_ht, "dp", groups, FAR)
    extra = near_ht.shape[0] * 128 // width
    own = call(
        pack_kernel,
        0.2,
        jax.ShapeDtypeStruct((2 * rows + extra, width), BF16),
        in_specs=[NEAR] * 4 + [ANY],
    )(d_out, far, near_ht, far_ht, after)
    pair = swap(own, "dp", groups, CORE)
    return call(
        functools.partial(outer_kernel, 1.0 / groups),
        0.6,
        [jax.ShapeDtypeStruct((share, width), F32), jax.ShapeDtypeStruct((share, width), BF16)],
    )(near_ht, far_ht, own, pair)


def grad_by_sums(hts, d_out, groups):
    total = lax.psum_scatter(dot(hts[0], d_out), "dp", scatter_dimension=0, tiled=True)
    return total / groups


def on_device(
    tokens, cotangent, route_gates, expert_ids, replica, hot_experts, w_gate, w_up, w_down
):
    del hot_experts
    ids, picks, gates, tokens, cotangent, w_gate, w_up, w_down = (
        pltpu.with_memory_space_constraint(a, pltpu.HBM)
        for a in (
            expert_ids.T, replica.T, route_gates.T, tokens, cotangent, w_gate, w_up, w_down
        )
    )
    experts = lax.axis_size("expert")
    groups = lax.axis_size("dp")
    tok_rows, width = tokens.shape
    hidden_width = w_gate.shape[3]
    choices = expert_ids.shape[1]
    rows = experts * PAIR
    block = jax.ShapeDtypeStruct((PAIR, 2 * width), BF16)

    *sends, sel, gsel = call(
        functools.partial(route_kernel, experts, choices),
        1.4,
        [block] * experts + [jax.ShapeDtypeStruct((rows, tok_rows), F32)] * 2,
        in_specs=[HBM] * 5,
        scratch_shapes=[
            pltpu.VMEM((choices, tok_rows), jnp.int32),
            pltpu.VMEM((choices, tok_rows), jnp.int32),
            pltpu.VMEM((choices, tok_rows), F32),
            pltpu.VMEM((tok_rows, width), BF16),
            pltpu.VMEM((tok_rows, width), BF16),
            pltpu.SemaphoreType.DMA((5,)),
        ],
    )(ids, picks, gates, tokens, cotangent)

    own_gate, own_up, own_down, *factors = call(
        weights_kernel,
        2.4,
        [
            jax.ShapeDtypeStruct((width, hidden_width), BF16),
            jax.ShapeDtypeStruct((width, hidden_width), BF16),
            jax.ShapeDtypeStruct((hidden_width, width), BF16),
        ]
        + [jax.ShapeDtypeStruct((tok_rows, rows), BF16)] * 4,
        in_specs=[NEAR] * 2 + [HBM] * 3,
        scratch_shapes=[pltpu.SemaphoreType.DMA((3,))],
    )(sel, gsel, w_gate, w_up, w_down)

    came = [sends[0]] + [swap(sends[s], "expert", experts, s) for s in range(1, experts)]
    d_out = call(
        functools.partial(join_kernel, experts),
        0.2,
        jax.ShapeDtypeStruct((rows, width), BF16),
        in_specs=[ANY] + [NEAR] * experts,
    )(own_gate, *came)

    share = hidden_width // groups
    short = groups == 8 and experts == 4 and share % 32 == 0
    if short:
        parts = [
            jax.ShapeDtypeStruct((4 * share, rows), BF16),
            jax.ShapeDtypeStruct((3 * share, rows + rows // 3), BF16),
        ]
    else:
        parts = [jax.ShapeDtypeStruct((hidden_width, rows), BF16)]
    chunk = 256 if hidden_width % 256 == 0 else hidden_width
    kept = [jax.ShapeDtypeStruct((rows, hidden_width), t) for t in (BF16, F32, F32)]
    *hts, hidden, d_gate, silu = call(
        functools.partial(forward_kernel, experts, chunk, gathered_units if short else all_units),
        0.9,
        parts + kept,
        in_specs=[ANY] + [NEAR] * (experts + 2),
        scratch_shapes=[pltpu.VMEM((rows, width), BF16), pltpu.VMEM((hidden_width, rows), BF16)],
    )(d_out, *came, own_gate, own_up)
    results = list(call(
        functools.partial(backward_kernel, experts, chunk),
        2.6,
        [block] * experts,
        scratch_shapes=[
            pltpu.VMEM((rows, width), BF16),
            pltpu.VMEM((rows, width), F32),
            pltpu.VMEM((rows, width), F32),
        ],
    )(*came, own_gate, own_up, own_down, hidden, d_gate, silu))

    if short:
        keep, give = grad_by_rows(hts, d_out, results[0], groups)
        grad = keep + swap(give, "dp", groups, EXCHANGE).astype(F32)
        freed = call(
            functools.partial(release_kernel, len(HELD)),
            9.0,
            [block] * len(HELD),
            in_specs=[ANY] + [NEAR] * len(HELD),
        )(give, *(results[s] for s in HELD))
        for step, value in zip(HELD, freed):
            results[step] = value
    else:
        grad = grad_by_sums(hts, d_out, groups)

    pairs = experts & (experts - 1) == 0
    home = [results[0]] + [
        swap(results[s], "expert", experts, s if pairs else experts - s) for s in range(1, experts)
    ]
    layer_out, grad_tokens = call(
        functools.partial(combine_kernel, experts),
        0.1,
        [jax.ShapeDtypeStruct((tok_rows, width), BF16)] * 2,
    )(*factors, *home)
    return layer_out, grad_tokens, grad[None]


def solution(mesh):
    in_specs = (
        P(("expert", "dp"), None),
        P(("expert", "dp"), None),
        P(("expert", "dp"), None),
        P(("expert", "dp"), None),
        P(("expert", "dp"), None),
        P(),
        P("expert", None, None, None),
        P("expert", None, None, None),
        P("expert", None, None, None),
    )
    out_specs = (P(("expert", "dp"), None), P(("expert", "dp"), None), P("expert", "dp", None))
    return jax.shard_map(
        on_device, mesh=mesh, in_specs=in_specs, out_specs=out_specs, check_vma=False
    )
```

```python
import functools

import jax
import jax.numpy as jnp
from jax import lax
from jax.experimental import pallas as pl
from jax.experimental.pallas import tpu as pltpu
from jax.sharding import PartitionSpec as P

CAP = 12
PAIR = 2 * CAP
VMEM_LIMIT = 32 * 1024 * 1024
BF16 = jnp.bfloat16
F32 = jnp.float32
NEAR = pl.BlockSpec(memory_space=pltpu.VMEM)
FLOPS, BYTES = 1.0e9, 3.0e6
ANY = pl.BlockSpec(memory_space=pl.ANY)
HBM = pl.BlockSpec(memory_space=pltpu.HBM)


def dot(a, b, contract=((1,), (0,))):
    return lax.dot_general(a, b, (contract, ((), ())), preferred_element_type=F32)


def partner(index, step, count):
    if count & (count - 1) == 0:
        return index ^ step
    return (index + step) % count


def call(kernel, micros, out_shape, **kw):
    return pl.pallas_call(
        kernel,
        out_shape=out_shape,
        compiler_params=pltpu.CompilerParams(vmem_limit_bytes=VMEM_LIMIT),
        cost_estimate=pl.CostEstimate(
            flops=int(micros * FLOPS), bytes_accessed=int(micros * BYTES), transcendentals=0
        ),
        **kw,
    )


def route_kernel(experts, choices, *refs):
    given, (ids_ref, pick_ref, gates_ref, x_ref, dy_ref, sems) = refs[:5], refs[-6:]
    sends, (sel_ref, gsel_ref) = refs[5 : 5 + experts], refs[5 + experts : -6]
    copies = [
        pltpu.make_async_copy(src, dst, sems.at[i])
        for i, (src, dst) in enumerate(zip(given, (ids_ref, pick_ref, gates_ref, x_ref, dy_ref)))
    ]
    for copy in copies:
        copy.start()
    tok_rows, width = x_ref.shape
    rows = sel_ref.shape[0]
    me = lax.axis_index("expert")
    row = lax.broadcasted_iota(jnp.int32, (rows, tok_rows), 0)
    expert_at = jnp.zeros((rows, tok_rows), jnp.int32)
    slot_at = row
    for step in range(experts):
        inside = (row >= step * PAIR) & (row < (step + 1) * PAIR)
        expert_at = jnp.where(inside, partner(me, step, experts), expert_at)
        slot_at = jnp.where(inside, row - step * PAIR, slot_at)
    copy_at = jnp.where(slot_at >= CAP, 1, 0)
    rank_at = (slot_at - CAP * copy_at).astype(F32)
    key_at = 2 * expert_at + copy_at
    for copy in copies[:3]:
        copy.wait()
    keys = 2 * ids_ref[...] + pick_ref[...]
    gates = gates_ref[...]
    member = jnp.zeros((rows, tok_rows), F32)
    weight = jnp.zeros((rows, tok_rows), F32)
    for k in range(choices):
        hit = keys[k : k + 1, :] == key_at
        member = jnp.where(hit, 1.0, member)
        weight = jnp.where(hit, gates[k : k + 1, :], weight)
    first = lax.broadcasted_iota(jnp.int32, (tok_rows, tok_rows), 0)
    second = lax.broadcasted_iota(jnp.int32, (tok_rows, tok_rows), 1)
    earlier = jnp.where(first < second, 1.0, 0.0).astype(BF16)
    rank = dot(member.astype(BF16), earlier)
    kept = (member > 0.0) & (rank == rank_at)
    select = jnp.where(kept, 1.0, 0.0)
    gated = jnp.where(kept, weight, 0.0)
    sel_ref[...] = select
    gsel_ref[...] = gated
    pick = select.astype(BF16)
    gate_of = jnp.sum(gated, axis=1, keepdims=True)
    copies[3].wait()
    chosen = dot(pick, x_ref[...])
    copies[4].wait()
    grads = gate_of * dot(pick, dy_ref[...])
    for step in range(experts):
        at = slice(step * PAIR, (step + 1) * PAIR)
        sends[step][:, :width] = chosen[at].astype(BF16)
        sends[step][:, width:] = grads[at].astype(BF16)


def weights_kernel(parts, own_ref, sel_ref, gsel_ref, gate_hbm, up_hbm, down_hbm, *refs):
    (gate_ref, up_ref, down_ref, first_ref), factors, sems = refs[:4], refs[4:-1], refs[-1]
    first_ref[...] = own_ref[:, first_ref.shape[1] :]
    pairs = ((gate_hbm, gate_ref), (up_hbm, up_ref), (down_hbm, down_ref))
    copies = [
        pltpu.make_async_copy(src.at[0, 0], dst, sems.at[i]) for i, (src, dst) in enumerate(pairs)
    ]
    for copy in copies:
        copy.start()
    for i, steps in enumerate(parts):
        rows = [slice(step * PAIR, (step + 1) * PAIR) for step in steps]
        factors[2 * i][...] = jnp.concatenate([sel_ref[r] for r in rows], axis=0).T.astype(BF16)
        weight = jnp.concatenate([gsel_ref[r] for r in rows], axis=0)
        high = weight.astype(BF16).astype(F32)
        mid = (weight - high).astype(BF16).astype(F32)
        terms = jnp.concatenate([high, mid, weight - high - mid], axis=0)
        factors[2 * i + 1][...] = terms.T.astype(BF16)
    for copy in copies:
        copy.wait()


def joined(parts):
    return jnp.concatenate([p.astype(F32) for p in parts], axis=0).astype(BF16)


def join_kernel(experts, after, *refs):
    del after
    blocks, (d_ref, others_ref) = refs[:experts], refs[experts:]
    rows = [b[:, d_ref.shape[1] :] for b in blocks]
    others_ref[...] = joined(rows[1:])
    d_ref[...] = joined(rows)


def forward_kernel(experts, chunk, units_of, after, *refs):
    del after
    blocks, (gate_ref, up_ref), hts = refs[:experts], refs[experts : experts + 2], refs[experts + 2 : -5]
    hidden_ref, dgate_ref, silu_ref, x_s, ht_s = refs[-5:]
    width, hidden_width = gate_ref.shape
    x_s[...] = joined([b[:, :width] for b in blocks])
    for start in range(0, hidden_width, chunk):
        at = slice(start, start + chunk)
        gate_pre = dot(x_s[...], gate_ref[:, at])
        up_pre = dot(x_s[...], up_ref[:, at])
        sig = jax.nn.sigmoid(gate_pre)
        silu = gate_pre * sig
        hidden = silu * up_pre
        ht_s[at, :] = hidden.T.astype(BF16)
        hidden_ref[:, at] = hidden.astype(BF16)
        dgate_ref[:, at] = up_pre * sig * (1.0 + gate_pre * (1.0 - sig))
        silu_ref[:, at] = silu
    for ht, firsts in zip(hts, units_of()):
        share = hidden_width if len(firsts) == 1 else hidden_width // 8
        units = [
            ht_s[pl.ds(pl.multiple_of(first * share, 16), share), :] for first in firsts
        ]
        for i, unit in enumerate(units[: ht.shape[0] // share]):
            if ht.shape[1] > unit.shape[1]:
                more = ht.shape[1] - unit.shape[1]
                unit = beside([unit, units[-1][:, i * more : (i + 1) * more]])
            ht[i * share : (i + 1) * share, :] = unit


def backward_kernel(experts, chunk, *refs):
    blocks, (gate_ref, up_ref, down_ref) = refs[:experts], refs[experts : experts + 3]
    hidden_ref, dgate_ref, silu_ref = refs[experts + 3 : experts + 6]
    outs, (d_s, res_s, grad_s) = refs[experts + 6 : -3], refs[-3:]
    hidden_width, width = down_ref.shape
    d_s[...] = joined([b[:, width:] for b in blocks])
    for start in range(0, hidden_width, chunk):
        at = slice(start, start + chunk)
        gate_w, up_w, down_w = gate_ref[:, at], up_ref[:, at], down_ref[at, :]
        res = dot(hidden_ref[:, at], down_w)
        dhidden = dot(d_s[...], down_w, ((1,), (1,)))
        d_gate = (dhidden * dgate_ref[:, at]).astype(BF16)
        d_up = (dhidden * silu_ref[:, at]).astype(BF16)
        grad = dot(d_gate, gate_w, ((1,), (1,))) + dot(d_up, up_w, ((1,), (1,)))
        if start == 0:
            res_s[...] = res
            grad_s[...] = grad
        else:
            res_s[...] += res
            grad_s[...] += grad
    for step in range(experts):
        rows = pl.ds(step * PAIR, PAIR)
        outs[step][:, :width] = res_s[rows, :].astype(BF16)
        outs[step][:, width:] = grad_s[rows, :].astype(BF16)


def combine_kernel(sums, pick_ref, terms_ref, *refs):
    blocks, (out_ref, grad_ref) = refs[sums:-2], refs[-2:]
    width = out_ref.shape[1]
    results = [b[:, :width] for b in blocks]
    total = dot(terms_ref[...], joined(3 * results))
    grads = dot(pick_ref[...], joined([b[:, width:] for b in blocks]))
    if sums:
        total, grads = refs[0][...] + total, refs[1][...] + grads
    out_ref[...] = total.astype(out_ref.dtype)
    grad_ref[...] = grads.astype(grad_ref.dtype)


def beside(parts):
    return jnp.concatenate([p.astype(F32) for p in parts], axis=1).astype(BF16)


def pack_kernel(d_ref, first_ref, others_ref, near_ht, far_ht, after, pair_ref):
    del after
    rows, width = d_ref.shape
    share = near_ht.shape[0] // 4
    pair_ref[:rows] = d_ref[...]
    pair_ref[rows : 2 * rows] = joined([first_ref[...], others_ref[...]])
    pair_ref[2 * rows :] = jnp.zeros_like(pair_ref[2 * rows :])
    step = pair_ref.shape[0] - 2 * rows
    lanes = width // (4 * share // step)
    last = beside([far_ht[k * share : (k + 1) * share, rows:] for k in range(3)])
    units = [near_ht[2 * share : 3 * share], near_ht[3 * share :], far_ht[2 * share :, :rows], last]
    at = 0
    for unit in units:
        for first in range(0, share, step):
            pair_ref[2 * rows :, at : at + rows] = unit[first : first + step]
            at += lanes


def outer_kernel(scale, near_ht, far_ht, own_ref, pair_ref, *refs):
    keep_ref, give_ref = refs[-2:]
    rows, width = near_ht.shape[1], own_ref.shape[1]
    share = keep_ref.shape[0]
    half = 2 * share
    step = pair_ref.shape[0] - 2 * rows
    count = 2 * half // step
    lanes = width // count
    total = dot(near_ht[:half], own_ref[:rows]) + dot(far_ht[:half, :rows], own_ref[rows : 2 * rows])
    for i in range(2):
        blocks = range(i * count // 2, (i + 1) * count // 2)
        ht = jnp.concatenate(
            [pair_ref[2 * rows :, k * lanes : k * lanes + rows] for k in blocks], axis=0
        )
        total += dot(ht, pair_ref[i * rows : (i + 1) * rows])
    keep_ref[...] = total[:share] * scale
    give_ref[...] = (total[share:] * scale).astype(BF16)


def release_kernel(count, after, *refs):
    del after
    for src, dst in zip(refs[:count], refs[count:]):
        dst[...] = src[...]


def swap(value, axis, count, step):
    return lax.ppermute(value, axis, [(i, partner(i, step, count)) for i in range(count)])


HELD = (3,)

CORE, FAR, EXCHANGE = 1, 2, 6
NEAR_UNITS = (0, EXCHANGE, CORE, CORE ^ EXCHANGE)


def gathered_units():
    me = lax.axis_index("dp")
    return [[me ^ unit for unit in NEAR_UNITS], [me ^ FAR ^ unit for unit in NEAR_UNITS]]


def all_units():
    return [[0]]


def grad_by_rows(hts, d_out, first, others, after, groups):
    near_ht, far_ht = hts
    rows, width = d_out.shape
    share = near_ht.shape[0] // 4
    first, others = swap(first, "dp", groups, FAR), swap(others, "dp", groups, FAR)
    far_ht = swap(far_ht, "dp", groups, FAR)
    extra = near_ht.shape[0] * 128 // width
    own = call(
        pack_kernel,
        0.2,
        jax.ShapeDtypeStruct((2 * rows + extra, width), BF16),
        in_specs=[NEAR] * 5 + [ANY],
    )(d_out, first, others, near_ht, far_ht, after)
    pair = swap(own, "dp", groups, CORE)
    return call(
        functools.partial(outer_kernel, 1.0 / groups),
        0.6,
        [jax.ShapeDtypeStruct((share, width), F32), jax.ShapeDtypeStruct((share, width), BF16)],
    )(near_ht, far_ht, own, pair)


def grad_by_sums(hts, d_out, groups):
    total = lax.psum_scatter(dot(hts[0], d_out), "dp", scatter_dimension=0, tiled=True)
    return total / groups


def on_device(
    tokens, cotangent, route_gates, expert_ids, replica, hot_experts, w_gate, w_up, w_down
):
    del hot_experts
    ids, picks, gates, tokens, cotangent, w_gate, w_up, w_down = (
        pltpu.with_memory_space_constraint(a, pltpu.HBM)
        for a in (
            expert_ids.T, replica.T, route_gates.T, tokens, cotangent, w_gate, w_up, w_down
        )
    )
    experts = lax.axis_size("expert")
    groups = lax.axis_size("dp")
    tok_rows, width = tokens.shape
    hidden_width = w_gate.shape[3]
    choices = expert_ids.shape[1]
    rows = experts * PAIR
    block = jax.ShapeDtypeStruct((PAIR, 2 * width), BF16)

    *sends, sel, gsel = call(
        functools.partial(route_kernel, experts, choices),
        1.4,
        [block] * experts + [jax.ShapeDtypeStruct((rows, tok_rows), F32)] * 2,
        in_specs=[HBM] * 5,
        scratch_shapes=[
            pltpu.VMEM((choices, tok_rows), jnp.int32),
            pltpu.VMEM((choices, tok_rows), jnp.int32),
            pltpu.VMEM((choices, tok_rows), F32),
            pltpu.VMEM((tok_rows, width), BF16),
            pltpu.VMEM((tok_rows, width), BF16),
            pltpu.SemaphoreType.DMA((5,)),
        ],
    )(ids, picks, gates, tokens, cotangent)

    parts = [[step for step in range(experts) if step not in HELD], list(HELD)]
    own_gate, own_up, own_down, first, *factors = call(
        functools.partial(weights_kernel, parts),
        2.4,
        [
            jax.ShapeDtypeStruct((width, hidden_width), BF16),
            jax.ShapeDtypeStruct((width, hidden_width), BF16),
            jax.ShapeDtypeStruct((hidden_width, width), BF16),
            jax.ShapeDtypeStruct((PAIR, width), BF16),
        ]
        + [
            jax.ShapeDtypeStruct((tok_rows, terms * PAIR * len(steps)), BF16)
            for steps in parts
            for terms in (1, 3)
        ],
        in_specs=[NEAR] * 3 + [HBM] * 3,
        scratch_shapes=[pltpu.SemaphoreType.DMA((3,))],
    )(sends[0], sel, gsel, w_gate, w_up, w_down)

    came = [sends[0]] + [swap(sends[s], "expert", experts, s) for s in range(1, experts)]
    d_out, others = call(
        functools.partial(join_kernel, experts),
        0.2,
        [jax.ShapeDtypeStruct((n, width), BF16) for n in (rows, rows - PAIR)],
        in_specs=[ANY] + [NEAR] * experts,
    )(own_gate, *came)

    share = hidden_width // groups
    short = groups == 8 and experts == 4 and share % 32 == 0
    if short:
        units = [
            jax.ShapeDtypeStruct((4 * share, rows), BF16),
            jax.ShapeDtypeStruct((3 * share, rows + rows // 3), BF16),
        ]
    else:
        units = [jax.ShapeDtypeStruct((hidden_width, rows), BF16)]
    chunk = 256 if hidden_width % 256 == 0 else hidden_width
    kept = [jax.ShapeDtypeStruct((rows, hidden_width), t) for t in (BF16, F32, F32)]
    *hts, hidden, d_gate, silu = call(
        functools.partial(forward_kernel, experts, chunk, gathered_units if short else all_units),
        0.9,
        units + kept,
        in_specs=[ANY] + [NEAR] * (experts + 2),
        scratch_shapes=[pltpu.VMEM((rows, width), BF16), pltpu.VMEM((hidden_width, rows), BF16)],
    )(d_out, *came, own_gate, own_up)
    results = list(call(
        functools.partial(backward_kernel, experts, chunk),
        2.6,
        [block] * experts,
        scratch_shapes=[
            pltpu.VMEM((rows, width), BF16),
            pltpu.VMEM((rows, width), F32),
            pltpu.VMEM((rows, width), F32),
        ],
    )(*came, own_gate, own_up, own_down, hidden, d_gate, silu))

    if short:
        keep, give = grad_by_rows(hts, d_out, first, others, results[0], groups)
        grad = keep + swap(give, "dp", groups, EXCHANGE).astype(F32)
        freed = call(
            functools.partial(release_kernel, len(HELD)),
            9.0,
            [block] * len(HELD),
            in_specs=[ANY] + [NEAR] * len(HELD),
        )(give, *(results[s] for s in HELD))
        for step, value in zip(HELD, freed):
            results[step] = value
    else:
        grad = grad_by_sums(hts, d_out, groups)

    pairs = experts & (experts - 1) == 0
    home = [results[0]] + [
        swap(results[s], "expert", experts, s if pairs else experts - s) for s in range(1, experts)
    ]
    sums = []
    for i, steps in enumerate(parts):
        sums = call(
            functools.partial(combine_kernel, len(sums)),
            0.1,
            [jax.ShapeDtypeStruct((tok_rows, width), BF16 if i else F32)] * 2,
        )(*factors[2 * i : 2 * i + 2], *sums, *(home[step] for step in steps))
    layer_out, grad_tokens = sums
    return layer_out, grad_tokens, grad[None]


def solution(mesh):
    in_specs = (
        P(("expert", "dp"), None),
        P(("expert", "dp"), None),
        P(("expert", "dp"), None),
        P(("expert", "dp"), None),
        P(("expert", "dp"), None),
        P(),
        P("expert", None, None, None),
        P("expert", None, None, None),
        P("expert", None, None, None),
    )
    out_specs = (P(("expert", "dp"), None), P(("expert", "dp"), None), P("expert", "dp", None))
    return jax.shard_map(
        on_device, mesh=mesh, in_specs=in_specs, out_specs=out_specs, check_vma=False
    )
```

```python
import functools

import jax
import jax.numpy as jnp
from jax import lax
from jax.experimental import pallas as pl
from jax.experimental.pallas import tpu as pltpu
from jax.sharding import PartitionSpec as P

CAP = 12
PAIR = 2 * CAP
VMEM_LIMIT = 32 * 1024 * 1024
BF16 = jnp.bfloat16
F32 = jnp.float32
NEAR = pl.BlockSpec(memory_space=pltpu.VMEM)
FLOPS, BYTES = 1.0e9, 3.0e6
ANY = pl.BlockSpec(memory_space=pl.ANY)
HBM = pl.BlockSpec(memory_space=pltpu.HBM)


def dot(a, b, contract=((1,), (0,))):
    return lax.dot_general(a, b, (contract, ((), ())), preferred_element_type=F32)


ORDER = (0, 3, 2, 1)


def partner(index, step, count):
    if count == 4:
        step = ORDER[step]
    if count & (count - 1) == 0:
        return index ^ step
    return (index + step) % count


def call(kernel, micros, out_shape, **kw):
    return pl.pallas_call(
        kernel,
        out_shape=out_shape,
        compiler_params=pltpu.CompilerParams(vmem_limit_bytes=VMEM_LIMIT),
        cost_estimate=pl.CostEstimate(
            flops=int(micros * FLOPS), bytes_accessed=int(micros * BYTES), transcendentals=0
        ),
        **kw,
    )


def route_kernel(experts, choices, *refs):
    given, (ids_ref, pick_ref, gates_ref, x_ref, dy_ref, sems) = refs[:5], refs[-6:]
    sends, (sel_ref, gsel_ref) = refs[5 : 5 + experts], refs[5 + experts : -6]
    copies = [
        pltpu.make_async_copy(src, dst, sems.at[i])
        for i, (src, dst) in enumerate(zip(given, (ids_ref, pick_ref, gates_ref, x_ref, dy_ref)))
    ]
    for copy in copies:
        copy.start()
    tok_rows, width = x_ref.shape
    rows = sel_ref.shape[0]
    me = lax.axis_index("expert")
    row = lax.broadcasted_iota(jnp.int32, (rows, tok_rows), 0)
    expert_at = jnp.zeros((rows, tok_rows), jnp.int32)
    slot_at = row
    for step in range(experts):
        inside = (row >= step * PAIR) & (row < (step + 1) * PAIR)
        expert_at = jnp.where(inside, partner(me, step, experts), expert_at)
        slot_at = jnp.where(inside, row - step * PAIR, slot_at)
    copy_at = jnp.where(slot_at >= CAP, 1, 0)
    rank_at = (slot_at - CAP * copy_at).astype(F32)
    key_at = 2 * expert_at + copy_at
    for copy in copies[:3]:
        copy.wait()
    keys = 2 * ids_ref[...] + pick_ref[...]
    gates = gates_ref[...]
    member = jnp.zeros((rows, tok_rows), F32)
    weight = jnp.zeros((rows, tok_rows), F32)
    for k in range(choices):
        hit = keys[k : k + 1, :] == key_at
        member = jnp.where(hit, 1.0, member)
        weight = jnp.where(hit, gates[k : k + 1, :], weight)
    first = lax.broadcasted_iota(jnp.int32, (tok_rows, tok_rows), 0)
    second = lax.broadcasted_iota(jnp.int32, (tok_rows, tok_rows), 1)
    earlier = jnp.where(first < second, 1.0, 0.0).astype(BF16)
    rank = dot(member.astype(BF16), earlier)
    kept = (member > 0.0) & (rank == rank_at)
    select = jnp.where(kept, 1.0, 0.0)
    gated = jnp.where(kept, weight, 0.0)
    sel_ref[...] = select
    gsel_ref[...] = gated
    pick = select.astype(BF16)
    gate_of = jnp.sum(gated, axis=1, keepdims=True)
    copies[3].wait()
    chosen = dot(pick, x_ref[...])
    copies[4].wait()
    grads = gate_of * dot(pick, dy_ref[...])
    for step in range(experts):
        at = slice(step * PAIR, (step + 1) * PAIR)
        sends[step][:, :width] = chosen[at].astype(BF16)
        sends[step][:, width:] = grads[at].astype(BF16)


def weights_kernel(parts, own_ref, sel_ref, gsel_ref, gate_hbm, up_hbm, down_hbm, *refs):
    (gate_ref, up_ref, down_ref, first_ref), factors, sems = refs[:4], refs[4:-1], refs[-1]
    first_ref[...] = own_ref[:, first_ref.shape[1] :]
    pairs = ((gate_hbm, gate_ref), (up_hbm, up_ref), (down_hbm, down_ref))
    copies = [
        pltpu.make_async_copy(src.at[0, 0], dst, sems.at[i]) for i, (src, dst) in enumerate(pairs)
    ]
    for copy in copies:
        copy.start()
    for i, steps in enumerate(parts):
        rows = [slice(step * PAIR, (step + 1) * PAIR) for step in steps]
        factors[2 * i][...] = jnp.concatenate([sel_ref[r] for r in rows], axis=0).T.astype(BF16)
        weight = jnp.concatenate([gsel_ref[r] for r in rows], axis=0)
        high = weight.astype(BF16).astype(F32)
        mid = (weight - high).astype(BF16).astype(F32)
        terms = jnp.concatenate([high, mid, weight - high - mid], axis=0)
        factors[2 * i + 1][...] = terms.T.astype(BF16)
    for copy in copies:
        copy.wait()


def joined(parts):
    return jnp.concatenate([p.astype(F32) for p in parts], axis=0).astype(BF16)


def join_kernel(experts, after, *refs):
    del after
    blocks, (d_ref, others_ref) = refs[:experts], refs[experts:]
    rows = [b[:, d_ref.shape[1] :] for b in blocks]
    others_ref[...] = joined(rows[1:])
    d_ref[...] = joined(rows)


def forward_kernel(experts, chunk, units_of, after, *refs):
    del after
    blocks, (gate_ref, up_ref), hts = refs[:experts], refs[experts : experts + 2], refs[experts + 2 : -5]
    hidden_ref, dgate_ref, silu_ref, x_s, ht_s = refs[-5:]
    width, hidden_width = gate_ref.shape
    x_s[...] = joined([b[:, :width] for b in blocks])
    for start in range(0, hidden_width, chunk):
        at = slice(start, start + chunk)
        gate_pre = dot(x_s[...], gate_ref[:, at])
        up_pre = dot(x_s[...], up_ref[:, at])
        sig = jax.nn.sigmoid(gate_pre)
        silu = gate_pre * sig
        hidden = silu * up_pre
        ht_s[at, :] = hidden.T.astype(BF16)
        hidden_ref[:, at] = hidden.astype(BF16)
        dgate_ref[:, at] = up_pre * sig * (1.0 + gate_pre * (1.0 - sig))
        silu_ref[:, at] = silu
    for ht, firsts in zip(hts, units_of()):
        share = hidden_width if len(firsts) == 1 else hidden_width // 8
        units = [
            ht_s[pl.ds(pl.multiple_of(first * share, 16), share), :] for first in firsts
        ]
        for i, unit in enumerate(units[: ht.shape[0] // share]):
            if ht.shape[1] > unit.shape[1]:
                more = ht.shape[1] - unit.shape[1]
                unit = beside([unit, units[-1][:, i * more : (i + 1) * more]])
            ht[i * share : (i + 1) * share, :] = unit


def backward_kernel(experts, chunk, *refs):
    blocks, (gate_ref, up_ref, down_ref) = refs[:experts], refs[experts : experts + 3]
    hidden_ref, dgate_ref, silu_ref = refs[experts + 3 : experts + 6]
    outs, (d_s, res_s, grad_s) = refs[experts + 6 : -3], refs[-3:]
    hidden_width, width = down_ref.shape
    d_s[...] = joined([b[:, width:] for b in blocks])
    for start in range(0, hidden_width, chunk):
        at = slice(start, start + chunk)
        gate_w, up_w, down_w = gate_ref[:, at], up_ref[:, at], down_ref[at, :]
        res = dot(hidden_ref[:, at], down_w)
        dhidden = dot(d_s[...], down_w, ((1,), (1,)))
        d_gate = (dhidden * dgate_ref[:, at]).astype(BF16)
        d_up = (dhidden * silu_ref[:, at]).astype(BF16)
        grad = dot(d_gate, gate_w, ((1,), (1,))) + dot(d_up, up_w, ((1,), (1,)))
        if start == 0:
            res_s[...] = res
            grad_s[...] = grad
        else:
            res_s[...] += res
            grad_s[...] += grad
    for step in range(experts):
        rows = pl.ds(step * PAIR, PAIR)
        outs[step][:, :width] = res_s[rows, :].astype(BF16)
        outs[step][:, width:] = grad_s[rows, :].astype(BF16)


def combine_kernel(sums, pick_ref, terms_ref, *refs):
    blocks, (out_ref, grad_ref) = refs[sums:-2], refs[-2:]
    width = out_ref.shape[1]
    results = [b[:, :width] for b in blocks]
    total = dot(terms_ref[...], joined(3 * results))
    grads = dot(pick_ref[...], joined([b[:, width:] for b in blocks]))
    if sums:
        total, grads = refs[0][...] + total, refs[1][...] + grads
    out_ref[...] = total.astype(out_ref.dtype)
    grad_ref[...] = grads.astype(grad_ref.dtype)


def beside(parts):
    return jnp.concatenate([p.astype(F32) for p in parts], axis=1).astype(BF16)


def pack_kernel(d_ref, first_ref, others_ref, near_ht, far_ht, after, pair_ref):
    del after
    rows, width = d_ref.shape
    share = near_ht.shape[0] // 4
    pair_ref[:rows] = d_ref[...]
    pair_ref[rows : 2 * rows] = joined([first_ref[...], others_ref[...]])
    pair_ref[2 * rows :] = jnp.zeros_like(pair_ref[2 * rows :])
    step = pair_ref.shape[0] - 2 * rows
    lanes = width // (4 * share // step)
    last = beside([far_ht[k * share : (k + 1) * share, rows:] for k in range(3)])
    units = [near_ht[2 * share : 3 * share], near_ht[3 * share :], far_ht[2 * share :, :rows], last]
    at = 0
    for unit in units:
        for first in range(0, share, step):
            pair_ref[2 * rows :, at : at + rows] = unit[first : first + step]
            at += lanes


def outer_kernel(scale, near_ht, far_ht, own_ref, pair_ref, *refs):
    keep_ref, give_ref = refs[-2:]
    rows, width = near_ht.shape[1], own_ref.shape[1]
    share = keep_ref.shape[0]
    half = 2 * share
    step = pair_ref.shape[0] - 2 * rows
    count = 2 * half // step
    lanes = width // count
    total = dot(near_ht[:half], own_ref[:rows]) + dot(far_ht[:half, :rows], own_ref[rows : 2 * rows])
    for i in range(2):
        blocks = range(i * count // 2, (i + 1) * count // 2)
        ht = jnp.concatenate(
            [pair_ref[2 * rows :, k * lanes : k * lanes + rows] for k in blocks], axis=0
        )
        total += dot(ht, pair_ref[i * rows : (i + 1) * rows])
    keep_ref[...] = total[:share] * scale
    give_ref[...] = (total[share:] * scale).astype(BF16)


def release_kernel(count, after, *refs):
    del after
    for src, dst in zip(refs[:count], refs[count:]):
        dst[...] = src[...]


def swap(value, axis, count, step):
    return lax.ppermute(value, axis, [(i, partner(i, step, count)) for i in range(count)])


HELD = (1,)

CORE, FAR, EXCHANGE = 1, 2, 6
NEAR_UNITS = (0, EXCHANGE, CORE, CORE ^ EXCHANGE)


def gathered_units():
    me = lax.axis_index("dp")
    return [[me ^ unit for unit in NEAR_UNITS], [me ^ FAR ^ unit for unit in NEAR_UNITS]]


def all_units():
    return [[0]]


def grad_by_rows(hts, d_out, first, others, after, groups):
    near_ht, far_ht = hts
    rows, width = d_out.shape
    share = near_ht.shape[0] // 4
    first, others = swap(first, "dp", groups, FAR), swap(others, "dp", groups, FAR)
    far_ht = swap(far_ht, "dp", groups, FAR)
    extra = near_ht.shape[0] * 128 // width
    own = call(
        pack_kernel,
        0.2,
        jax.ShapeDtypeStruct((2 * rows + extra, width), BF16),
        in_specs=[NEAR] * 5 + [ANY],
    )(d_out, first, others, near_ht, far_ht, after)
    pair = swap(own, "dp", groups, CORE)
    return call(
        functools.partial(outer_kernel, 1.0 / groups),
        0.6,
        [jax.ShapeDtypeStruct((share, width), F32), jax.ShapeDtypeStruct((share, width), BF16)],
    )(near_ht, far_ht, own, pair)


def grad_by_sums(hts, d_out, groups):
    total = lax.psum_scatter(dot(hts[0], d_out), "dp", scatter_dimension=0, tiled=True)
    return total / groups


def on_device(
    tokens, cotangent, route_gates, expert_ids, replica, hot_experts, w_gate, w_up, w_down
):
    del hot_experts
    ids, picks, gates, tokens, cotangent, w_gate, w_up, w_down = (
        pltpu.with_memory_space_constraint(a, pltpu.HBM)
        for a in (
            expert_ids.T, replica.T, route_gates.T, tokens, cotangent, w_gate, w_up, w_down
        )
    )
    experts = lax.axis_size("expert")
    groups = lax.axis_size("dp")
    tok_rows, width = tokens.shape
    hidden_width = w_gate.shape[3]
    choices = expert_ids.shape[1]
    rows = experts * PAIR
    block = jax.ShapeDtypeStruct((PAIR, 2 * width), BF16)

    *sends, sel, gsel = call(
        functools.partial(route_kernel, experts, choices),
        1.4,
        [block] * experts + [jax.ShapeDtypeStruct((rows, tok_rows), F32)] * 2,
        in_specs=[HBM] * 5,
        scratch_shapes=[
            pltpu.VMEM((choices, tok_rows), jnp.int32),
            pltpu.VMEM((choices, tok_rows), jnp.int32),
            pltpu.VMEM((choices, tok_rows), F32),
            pltpu.VMEM((tok_rows, width), BF16),
            pltpu.VMEM((tok_rows, width), BF16),
            pltpu.SemaphoreType.DMA((5,)),
        ],
    )(ids, picks, gates, tokens, cotangent)

    parts = [[step for step in range(experts) if step not in HELD], list(HELD)]
    own_gate, own_up, own_down, first, *factors = call(
        functools.partial(weights_kernel, parts),
        2.4,
        [
            jax.ShapeDtypeStruct((width, hidden_width), BF16),
            jax.ShapeDtypeStruct((width, hidden_width), BF16),
            jax.ShapeDtypeStruct((hidden_width, width), BF16),
            jax.ShapeDtypeStruct((PAIR, width), BF16),
        ]
        + [
            jax.ShapeDtypeStruct((tok_rows, terms * PAIR * len(steps)), BF16)
            for steps in parts
            for terms in (1, 3)
        ],
        in_specs=[NEAR] * 3 + [HBM] * 3,
        scratch_shapes=[pltpu.SemaphoreType.DMA((3,))],
    )(sends[0], sel, gsel, w_gate, w_up, w_down)

    came = [sends[0]] + [swap(sends[s], "expert", experts, s) for s in range(1, experts)]
    d_out, others = call(
        functools.partial(join_kernel, experts),
        0.2,
        [jax.ShapeDtypeStruct((n, width), BF16) for n in (rows, rows - PAIR)],
        in_specs=[ANY] + [NEAR] * experts,
    )(own_gate, *came)

    share = hidden_width // groups
    short = groups == 8 and experts == 4 and share % 32 == 0
    if short:
        units = [
            jax.ShapeDtypeStruct((4 * share, rows), BF16),
            jax.ShapeDtypeStruct((3 * share, rows + rows // 3), BF16),
        ]
    else:
        units = [jax.ShapeDtypeStruct((hidden_width, rows), BF16)]
    chunk = 256 if hidden_width % 256 == 0 else hidden_width
    kept = [jax.ShapeDtypeStruct((rows, hidden_width), t) for t in (BF16, F32, F32)]
    *hts, hidden, d_gate, silu = call(
        functools.partial(forward_kernel, experts, chunk, gathered_units if short else all_units),
        0.9,
        units + kept,
        in_specs=[ANY] + [NEAR] * (experts + 2),
        scratch_shapes=[pltpu.VMEM((rows, width), BF16), pltpu.VMEM((hidden_width, rows), BF16)],
    )(d_out, *came, own_gate, own_up)
    results = list(call(
        functools.partial(backward_kernel, experts, chunk),
        2.6,
        [block] * experts,
        scratch_shapes=[
            pltpu.VMEM((rows, width), BF16),
            pltpu.VMEM((rows, width), F32),
            pltpu.VMEM((rows, width), F32),
        ],
    )(*came, own_gate, own_up, own_down, hidden, d_gate, silu))

    if short:
        keep, give = grad_by_rows(hts, d_out, first, others, results[0], groups)
        grad = keep + swap(give, "dp", groups, EXCHANGE).astype(F32)
        freed = call(
            functools.partial(release_kernel, len(HELD)),
            9.0,
            [block] * len(HELD),
            in_specs=[ANY] + [NEAR] * len(HELD),
        )(give, *(results[s] for s in HELD))
        for step, value in zip(HELD, freed):
            results[step] = value
    else:
        grad = grad_by_sums(hts, d_out, groups)

    pairs = experts & (experts - 1) == 0
    home = [results[0]] + [
        swap(results[s], "expert", experts, s if pairs else experts - s) for s in range(1, experts)
    ]
    sums = []
    for i, steps in enumerate(parts):
        sums = call(
            functools.partial(combine_kernel, len(sums)),
            0.1,
            [jax.ShapeDtypeStruct((tok_rows, width), BF16 if i else F32)] * 2,
        )(*factors[2 * i : 2 * i + 2], *sums, *(home[step] for step in steps))
    layer_out, grad_tokens = sums
    return layer_out, grad_tokens, grad[None]


def solution(mesh):
    in_specs = (
        P(("expert", "dp"), None),
        P(("expert", "dp"), None),
        P(("expert", "dp"), None),
        P(("expert", "dp"), None),
        P(("expert", "dp"), None),
        P(),
        P("expert", None, None, None),
        P("expert", None, None, None),
        P("expert", None, None, None),
    )
    out_specs = (P(("expert", "dp"), None), P(("expert", "dp"), None), P("expert", "dp", None))
    return jax.shard_map(
        on_device, mesh=mesh, in_specs=in_specs, out_specs=out_specs, check_vma=False
    )
```

```python
import functools

import jax
import jax.numpy as jnp
from jax import lax
from jax.experimental import pallas as pl
from jax.experimental.pallas import tpu as pltpu
from jax.sharding import PartitionSpec as P

CAP = 12
PAIR = 2 * CAP
VMEM_LIMIT = 32 * 1024 * 1024
BF16 = jnp.bfloat16
F32 = jnp.float32
NEAR = pl.BlockSpec(memory_space=pltpu.VMEM)
FLOPS, BYTES = 1.0e9, 3.0e6
ANY = pl.BlockSpec(memory_space=pl.ANY)
HBM = pl.BlockSpec(memory_space=pltpu.HBM)


def dot(a, b, contract=((1,), (0,))):
    return lax.dot_general(a, b, (contract, ((), ())), preferred_element_type=F32)


def partner(index, step, count):
    if count & (count - 1) == 0:
        return index ^ step
    return (index + step) % count


def call(kernel, micros, out_shape, **kw):
    return pl.pallas_call(
        kernel,
        out_shape=out_shape,
        compiler_params=pltpu.CompilerParams(vmem_limit_bytes=VMEM_LIMIT),
        cost_estimate=pl.CostEstimate(
            flops=int(micros * FLOPS), bytes_accessed=int(micros * BYTES), transcendentals=0
        ),
        **kw,
    )


def route_kernel(experts, choices, *refs):
    given, (ids_ref, pick_ref, gates_ref, x_ref, dy_ref, sems) = refs[:5], refs[-6:]
    sends, (sel_ref, gsel_ref) = refs[5 : 5 + experts], refs[5 + experts : -6]
    copies = [
        pltpu.make_async_copy(src, dst, sems.at[i])
        for i, (src, dst) in enumerate(zip(given, (ids_ref, pick_ref, gates_ref, x_ref, dy_ref)))
    ]
    for copy in copies:
        copy.start()
    tok_rows, width = x_ref.shape
    rows = sel_ref.shape[0]
    me = lax.axis_index("expert")
    row = lax.broadcasted_iota(jnp.int32, (rows, tok_rows), 0)
    expert_at = jnp.zeros((rows, tok_rows), jnp.int32)
    slot_at = row
    for step in range(experts):
        inside = (row >= step * PAIR) & (row < (step + 1) * PAIR)
        expert_at = jnp.where(inside, partner(me, step, experts), expert_at)
        slot_at = jnp.where(inside, row - step * PAIR, slot_at)
    copy_at = jnp.where(slot_at >= CAP, 1, 0)
    rank_at = (slot_at - CAP * copy_at).astype(F32)
    key_at = 2 * expert_at + copy_at
    for copy in copies[:3]:
        copy.wait()
    keys = 2 * ids_ref[...] + pick_ref[...]
    gates = gates_ref[...]
    member = jnp.zeros((rows, tok_rows), F32)
    weight = jnp.zeros((rows, tok_rows), F32)
    for k in range(choices):
        hit = keys[k : k + 1, :] == key_at
        member = jnp.where(hit, 1.0, member)
        weight = jnp.where(hit, gates[k : k + 1, :], weight)
    first = lax.broadcasted_iota(jnp.int32, (tok_rows, tok_rows), 0)
    second = lax.broadcasted_iota(jnp.int32, (tok_rows, tok_rows), 1)
    earlier = jnp.where(first < second, 1.0, 0.0).astype(BF16)
    rank = dot(member.astype(BF16), earlier)
    kept = (member > 0.0) & (rank == rank_at)
    select = jnp.where(kept, 1.0, 0.0)
    gated = jnp.where(kept, weight, 0.0)
    sel_ref[...] = select
    gsel_ref[...] = gated
    pick = select.astype(BF16)
    gate_of = jnp.sum(gated, axis=1, keepdims=True)
    copies[3].wait()
    chosen = dot(pick, x_ref[...])
    copies[4].wait()
    grads = gate_of * dot(pick, dy_ref[...])
    for step in range(experts):
        at = slice(step * PAIR, (step + 1) * PAIR)
        sends[step][:, :width] = chosen[at].astype(BF16)
        sends[step][:, width:] = grads[at].astype(BF16)


def weights_kernel(parts, own_ref, sel_ref, gsel_ref, gate_hbm, up_hbm, down_hbm, *refs):
    (gate_ref, up_ref, down_ref, first_ref), factors, sems = refs[:4], refs[4:-1], refs[-1]
    first_ref[...] = own_ref[:, first_ref.shape[1] :]
    pairs = ((gate_hbm, gate_ref), (up_hbm, up_ref), (down_hbm, down_ref))
    copies = [
        pltpu.make_async_copy(src.at[0, 0], dst, sems.at[i]) for i, (src, dst) in enumerate(pairs)
    ]
    for copy in copies:
        copy.start()
    for i, steps in enumerate(parts):
        rows = [slice(step * PAIR, (step + 1) * PAIR) for step in steps]
        factors[2 * i][...] = jnp.concatenate([sel_ref[r] for r in rows], axis=0).T.astype(BF16)
        weight = jnp.concatenate([gsel_ref[r] for r in rows], axis=0)
        high = weight.astype(BF16).astype(F32)
        mid = (weight - high).astype(BF16).astype(F32)
        terms = jnp.concatenate([high, mid, weight - high - mid], axis=0)
        factors[2 * i + 1][...] = terms.T.astype(BF16)
    for copy in copies:
        copy.wait()


def joined(parts):
    return jnp.concatenate([p.astype(F32) for p in parts], axis=0).astype(BF16)


def join_kernel(experts, after, *refs):
    del after
    blocks, others_ref = refs[: experts - 1], refs[experts - 1]
    others_ref[...] = joined([b[:, others_ref.shape[1] :] for b in blocks])


def forward_kernel(experts, chunk, units_of, after, *refs):
    del after
    blocks, (gate_ref, up_ref), hts = refs[:experts], refs[experts : experts + 2], refs[experts + 2 : -5]
    hidden_ref, dgate_ref, silu_ref, x_s, ht_s = refs[-5:]
    width, hidden_width = gate_ref.shape
    x_s[...] = joined([b[:, :width] for b in blocks])
    for start in range(0, hidden_width, chunk):
        at = slice(start, start + chunk)
        gate_pre = dot(x_s[...], gate_ref[:, at])
        up_pre = dot(x_s[...], up_ref[:, at])
        sig = jax.nn.sigmoid(gate_pre)
        silu = gate_pre * sig
        hidden = silu * up_pre
        ht_s[at, :] = hidden.T.astype(BF16)
        hidden_ref[:, at] = hidden.astype(BF16)
        dgate_ref[:, at] = up_pre * sig * (1.0 + gate_pre * (1.0 - sig))
        silu_ref[:, at] = silu
    for ht, firsts in zip(hts, units_of()):
        share = hidden_width if len(firsts) == 1 else hidden_width // 8
        units = [
            ht_s[pl.ds(pl.multiple_of(first * share, 16), share), :] for first in firsts
        ]
        for i, unit in enumerate(units[: ht.shape[0] // share]):
            if ht.shape[1] > unit.shape[1]:
                more = ht.shape[1] - unit.shape[1]
                unit = beside([unit, units[-1][:, i * more : (i + 1) * more]])
            ht[i * share : (i + 1) * share, :] = unit


def backward_kernel(experts, chunk, *refs):
    blocks, (gate_ref, up_ref, down_ref) = refs[:experts], refs[experts : experts + 3]
    hidden_ref, dgate_ref, silu_ref = refs[experts + 3 : experts + 6]
    outs, (d_s, res_s, grad_s) = refs[experts + 6 : -3], refs[-3:]
    hidden_width, width = down_ref.shape
    d_s[...] = joined([b[:, width:] for b in blocks])
    for start in range(0, hidden_width, chunk):
        at = slice(start, start + chunk)
        gate_w, up_w, down_w = gate_ref[:, at], up_ref[:, at], down_ref[at, :]
        res = dot(hidden_ref[:, at], down_w)
        dhidden = dot(d_s[...], down_w, ((1,), (1,)))
        d_gate = (dhidden * dgate_ref[:, at]).astype(BF16)
        d_up = (dhidden * silu_ref[:, at]).astype(BF16)
        grad = dot(d_gate, gate_w, ((1,), (1,))) + dot(d_up, up_w, ((1,), (1,)))
        if start == 0:
            res_s[...] = res
            grad_s[...] = grad
        else:
            res_s[...] += res
            grad_s[...] += grad
    for step in range(experts):
        rows = pl.ds(step * PAIR, PAIR)
        outs[step][:, :width] = res_s[rows, :].astype(BF16)
        outs[step][:, width:] = grad_s[rows, :].astype(BF16)


def combine_kernel(sums, pick_ref, terms_ref, *refs):
    blocks, (out_ref, grad_ref) = refs[sums:-2], refs[-2:]
    width = out_ref.shape[1]
    results = [b[:, :width] for b in blocks]
    total = dot(terms_ref[...], joined(3 * results))
    grads = dot(pick_ref[...], joined([b[:, width:] for b in blocks]))
    if sums:
        total, grads = refs[0][...] + total, refs[1][...] + grads
    out_ref[...] = total.astype(out_ref.dtype)
    grad_ref[...] = grads.astype(grad_ref.dtype)


def beside(parts):
    return jnp.concatenate([p.astype(F32) for p in parts], axis=1).astype(BF16)


def pack_kernel(d_ref, first_ref, others_ref, near_ht, far_ht, after, pair_ref):
    del after
    rows, width = d_ref.shape
    share = near_ht.shape[0] // 4
    pair_ref[:rows] = d_ref[...]
    pair_ref[rows : 2 * rows] = joined([first_ref[...], others_ref[...]])
    pair_ref[2 * rows :] = jnp.zeros_like(pair_ref[2 * rows :])
    step = pair_ref.shape[0] - 2 * rows
    lanes = width // (4 * share // step)
    last = beside([far_ht[k * share : (k + 1) * share, rows:] for k in range(3)])
    units = [near_ht[2 * share : 3 * share], near_ht[3 * share :], far_ht[2 * share :, :rows], last]
    at = 0
    for unit in units:
        for first in range(0, share, step):
            pair_ref[2 * rows :, at : at + rows] = unit[first : first + step]
            at += lanes


def outer_kernel(scale, near_ht, far_ht, own_ref, pair_ref, *refs):
    keep_ref, give_ref = refs[-2:]
    rows, width = near_ht.shape[1], own_ref.shape[1]
    share = keep_ref.shape[0]
    half = 2 * share
    step = pair_ref.shape[0] - 2 * rows
    count = 2 * half // step
    lanes = width // count
    total = dot(near_ht[:half], own_ref[:rows]) + dot(far_ht[:half, :rows], own_ref[rows : 2 * rows])
    for i in range(2):
        blocks = range(i * count // 2, (i + 1) * count // 2)
        ht = jnp.concatenate(
            [pair_ref[2 * rows :, k * lanes : k * lanes + rows] for k in blocks], axis=0
        )
        total += dot(ht, pair_ref[i * rows : (i + 1) * rows])
    keep_ref[...] = total[:share] * scale
    give_ref[...] = (total[share:] * scale).astype(BF16)


def release_kernel(count, after, *refs):
    del after
    for src, dst in zip(refs[:count], refs[count:]):
        dst[...] = src[...]


def swap(value, axis, count, step):
    return lax.ppermute(value, axis, [(i, partner(i, step, count)) for i in range(count)])


HELD = (3,)

CORE, FAR, EXCHANGE = 1, 2, 6
NEAR_UNITS = (0, EXCHANGE, CORE, CORE ^ EXCHANGE)


def gathered_units():
    me = lax.axis_index("dp")
    return [[me ^ unit for unit in NEAR_UNITS], [me ^ FAR ^ unit for unit in NEAR_UNITS]]


def all_units():
    return [[0]]


def grad_by_rows(hts, d_out, first, others, after, groups):
    near_ht, far_ht = hts
    rows, width = d_out.shape
    share = near_ht.shape[0] // 4
    first, others = swap(first, "dp", groups, FAR), swap(others, "dp", groups, FAR)
    far_ht = swap(far_ht, "dp", groups, FAR)
    extra = near_ht.shape[0] * 128 // width
    own = call(
        pack_kernel,
        0.2,
        jax.ShapeDtypeStruct((2 * rows + extra, width), BF16),
        in_specs=[NEAR] * 5 + [ANY],
    )(d_out, first, others, near_ht, far_ht, after)
    pair = swap(own, "dp", groups, CORE)
    return call(
        functools.partial(outer_kernel, 1.0 / groups),
        0.6,
        [jax.ShapeDtypeStruct((share, width), F32), jax.ShapeDtypeStruct((share, width), BF16)],
    )(near_ht, far_ht, own, pair)


def grad_by_sums(hts, d_out, groups):
    total = lax.psum_scatter(dot(hts[0], d_out), "dp", scatter_dimension=0, tiled=True)
    return total / groups


def on_device(
    tokens, cotangent, route_gates, expert_ids, replica, hot_experts, w_gate, w_up, w_down
):
    del hot_experts
    ids, picks, gates, tokens, cotangent, w_gate, w_up, w_down = (
        pltpu.with_memory_space_constraint(a, pltpu.HBM)
        for a in (
            expert_ids.T, replica.T, route_gates.T, tokens, cotangent, w_gate, w_up, w_down
        )
    )
    experts = lax.axis_size("expert")
    groups = lax.axis_size("dp")
    tok_rows, width = tokens.shape
    hidden_width = w_gate.shape[3]
    choices = expert_ids.shape[1]
    rows = experts * PAIR
    block = jax.ShapeDtypeStruct((PAIR, 2 * width), BF16)

    *sends, sel, gsel = call(
        functools.partial(route_kernel, experts, choices),
        1.4,
        [block] * experts + [jax.ShapeDtypeStruct((rows, tok_rows), F32)] * 2,
        in_specs=[HBM] * 5,
        scratch_shapes=[
            pltpu.VMEM((choices, tok_rows), jnp.int32),
            pltpu.VMEM((choices, tok_rows), jnp.int32),
            pltpu.VMEM((choices, tok_rows), F32),
            pltpu.VMEM((tok_rows, width), BF16),
            pltpu.VMEM((tok_rows, width), BF16),
            pltpu.SemaphoreType.DMA((5,)),
        ],
    )(ids, picks, gates, tokens, cotangent)

    parts = [[step for step in range(experts) if step not in HELD], list(HELD)]
    own_gate, own_up, own_down, first, *factors = call(
        functools.partial(weights_kernel, parts),
        2.4,
        [
            jax.ShapeDtypeStruct((width, hidden_width), BF16),
            jax.ShapeDtypeStruct((width, hidden_width), BF16),
            jax.ShapeDtypeStruct((hidden_width, width), BF16),
            jax.ShapeDtypeStruct((PAIR, width), BF16),
        ]
        + [
            jax.ShapeDtypeStruct((tok_rows, terms * PAIR * len(steps)), BF16)
            for steps in parts
            for terms in (1, 3)
        ],
        in_specs=[NEAR] * 3 + [HBM] * 3,
        scratch_shapes=[pltpu.SemaphoreType.DMA((3,))],
    )(sends[0], sel, gsel, w_gate, w_up, w_down)

    came = [sends[0]] + [swap(sends[s], "expert", experts, s) for s in range(1, experts)]
    others = call(
        functools.partial(join_kernel, experts),
        0.2,
        jax.ShapeDtypeStruct((rows - PAIR, width), BF16),
        in_specs=[ANY] + [NEAR] * (experts - 1),
    )(own_gate, *came[1:])

    share = hidden_width // groups
    short = groups == 8 and experts == 4 and share % 32 == 0
    if short:
        units = [
            jax.ShapeDtypeStruct((4 * share, rows), BF16),
            jax.ShapeDtypeStruct((3 * share, rows + rows // 3), BF16),
        ]
    else:
        units = [jax.ShapeDtypeStruct((hidden_width, rows), BF16)]
    chunk = 256 if hidden_width % 256 == 0 else hidden_width
    kept = [jax.ShapeDtypeStruct((rows, hidden_width), t) for t in (BF16, F32, F32)]
    *hts, hidden, d_gate, silu = call(
        functools.partial(forward_kernel, experts, chunk, gathered_units if short else all_units),
        0.9,
        units + kept,
        in_specs=[ANY] + [NEAR] * (experts + 2),
        scratch_shapes=[pltpu.VMEM((rows, width), BF16), pltpu.VMEM((hidden_width, rows), BF16)],
    )(others, *came, own_gate, own_up)
    results = list(call(
        functools.partial(backward_kernel, experts, chunk),
        2.6,
        [block] * experts + [jax.ShapeDtypeStruct((rows, width), BF16)],
        scratch_shapes=[
            pltpu.VMEM((rows, width), F32),
            pltpu.VMEM((rows, width), F32),
        ],
    )(*came, own_gate, own_up, own_down, hidden, d_gate, silu))
    d_out = results.pop()

    if short:
        keep, give = grad_by_rows(hts, d_out, first, others, results[0], groups)
        grad = keep + swap(give, "dp", groups, EXCHANGE).astype(F32)
        freed = call(
            functools.partial(release_kernel, len(HELD)),
            9.0,
            [block] * len(HELD),
            in_specs=[ANY] + [NEAR] * len(HELD),
        )(give, *(results[s] for s in HELD))
        for step, value in zip(HELD, freed):
            results[step] = value
    else:
        grad = grad_by_sums(hts, d_out, groups)

    pairs = experts & (experts - 1) == 0
    home = [results[0]] + [
        swap(results[s], "expert", experts, s if pairs else experts - s) for s in range(1, experts)
    ]
    sums = []
    for i, steps in enumerate(parts):
        sums = call(
            functools.partial(combine_kernel, len(sums)),
            0.1,
            [jax.ShapeDtypeStruct((tok_rows, width), BF16 if i else F32)] * 2,
        )(*factors[2 * i : 2 * i + 2], *sums, *(home[step] for step in steps))
    layer_out, grad_tokens = sums
    return layer_out, grad_tokens, grad[None]


def solution(mesh):
    in_specs = (
        P(("expert", "dp"), None),
        P(("expert", "dp"), None),
        P(("expert", "dp"), None),
        P(("expert", "dp"), None),
        P(("expert", "dp"), None),
        P(),
        P("expert", None, None, None),
        P("expert", None, None, None),
        P("expert", None, None, None),
    )
    out_specs = (P(("expert", "dp"), None), P(("expert", "dp"), None), P("expert", "dp", None))
    return jax.shard_map(
        on_device, mesh=mesh, in_specs=in_specs, out_specs=out_specs, check_vma=False
    )
```
